32 devices in a mesh: wide: 8 (over z, y), narrow: 4 (over x, core).
Axes of the slice: x: 2, y: 2, z: 4, core: 2. Of those that a mesh axis runs over, the one named last changes fastest.
Arguments:
- trace_guess: float32 [8, 4, 16, 128, 128], P('wide', 'narrow'), may hold values from -6 to 6
- trace_rhs: float32 [8, 4, 16, 128, 128], P('wide', 'narrow'), may hold values from -6 to 6
- block_inverse: bfloat16 [8, 4, 16, 128, 128], P('wide', 'narrow')
- coupling: bfloat16 [8, 4, 16, 2, 128, 128], P('wide', 'narrow'), may hold values from -0.1875 to 0.1875
- block_neighbours: int32 [8, 4, 16, 2], P('wide', 'narrow'), may hold values from 0 to 23
- block_send: int32 [8, 4, 4, 2], P('wide', 'narrow'), may hold values from 0 to 15
- cell_faces: int32 [8, 4, 6, 2048], P('wide', 'narrow'), may hold values from 0 to 3071
- face_coeff: float32 [8, 4, 6, 2048], P('wide', 'narrow'), may hold values from 0.2 to 2
- cell_source: float32 [8, 4, 2048], P('wide', 'narrow'), may hold values from -6 to 6
- cell_neighbours: int32 [8, 4, 6, 2048], P('wide', 'narrow'), may hold values from 0 to 3071, as said below
- upwind_flags: int32 [8, 4, 6, 2048], P('wide', 'narrow'), may hold values 0 or 1
- cell_send: int32 [8, 4, 4, 256], P('wide', 'narrow'), may hold values from 0 to 2047
- saturation: float32 [8, 4, 4, 2048], P('wide', 'narrow'), may hold values from -3 to 3
- step_ratio: float32 [8, 4, 2048], P('wide', 'narrow'), may hold values from 0.05 to 0.2
Outputs:
- traces: float32 [8, 4, 16, 128, 128], P('wide', 'narrow')
- saturation_next: float32 [8, 4, 4, 2048], P('wide', 'narrow')
The draws below stay inside these ranges and needn't reach their ends.
Inputs may be any that keep to these rules, and one draw needn't show every extreme that they name: `cell_neighbours`: faces 0 to 3 (f) index either an own cell (below 2048) or a cell of their own side's range, 2048 + f * 256 to 2048 + (f + 1) * 256 - 1; faces 4 and 5 index own cells only.
All inputs are finite; a program needn't handle non-finite values. No bound on the sum of `upwind_flags` on one device may be relied on, other than what follows from the above.
Results may differ from the reference program's by a relative error of at most 0.003.
Values may be sent and summed in bfloat16 or wider, within the bound.
No kernel may reach another device: no remote copies, remote signals or barrier semaphores. Data moves between devices by JAX's collectives and lax.ppermute only.
A program may use at most 64 MiB of HBM per device.

```python
import math
import jax
import jax.numpy as jnp
from jax import lax

F = 128
NB = 16
HB = 2
K = 2
R = 128
NC = 2048
HC = 256
N_WIDE = 8
N_NARROW = 4


def draw_block_inverse(key, part):
    first, second = jax.random.split(jax.random.fold_in(key, 11))
    shape = (N_WIDE, N_NARROW, NB, F, F)
    diagonal = jnp.exp(jax.random.uniform(first, shape[:-1], jnp.float32, math.log(0.15), math.log(0.6)))
    off_part = jax.random.normal(second, shape, jnp.float32) * (0.3 / math.sqrt(F))
    identity = (lax.broadcasted_iota(jnp.int32, (F, F), 0) == lax.broadcasted_iota(jnp.int32, (F, F), 1)).astype(jnp.float32)
    return (off_part + identity * diagonal[..., None]).astype(jnp.bfloat16)


def draw_cell_neighbours(key, part):
    first, second, third = jax.random.split(jax.random.fold_in(key, 23), 3)
    shape = (N_WIDE, N_NARROW, 6, NC)
    local = jax.random.randint(first, shape, 0, NC)
    offset = jax.random.randint(second, shape, 0, HC)
    face = lax.broadcasted_iota(jnp.int32, shape, 2)
    chosen = jax.random.randint(third, shape, 0, 2) * (face < 4).astype(jnp.int32)
    remote = NC + face * HC + offset
    return jnp.where(chosen == 1, remote, local).astype(jnp.int32)


def plant(result, own_key, least, high):
    longest = result.shape.index(max(result.shape))
    spots = []
    for shift in (0, 1):
        where = [jax.random.randint(jax.random.fold_in(own_key, axis), (), 0, length) for axis, length in enumerate(result.shape)]
        where[longest] = (where[longest] + shift) % result.shape[longest]
        spots.append(tuple(where))
    return result.at[spots[0]].set(least).at[spots[1]].set(high)


def steps_of(rng, shape, shards, least, largest):
    level, own = 1.0, jax.random.fold_in(rng, 6)
    for axis_at, parts in shards:
        steps = jnp.exp(jax.random.uniform(jax.random.fold_in(own, axis_at), (parts,), jnp.float32, least / len(shards), largest / len(shards)))
        level = level * jnp.repeat(steps, shape[axis_at] // parts).reshape([-1 if axis == axis_at else 1 for axis in range(len(shape))])
    return level


def gaussian(own_key, dims, spread, reach, shards=(), kind=jnp.bfloat16):
    values = spread * jax.random.normal(own_key, dims, jnp.float32)
    if shards:
        values = values * steps_of(own_key, dims, shards, -0.22, 0.18)
    return jnp.clip(values, -reach, reach).astype(kind)


def setup_inputs(seed: int = 0) -> dict:
    streams_of = jax.random.split(jax.random.key(seed), 15)
    trace_guess = gaussian(streams_of[0], (N_WIDE, N_NARROW, NB, R, F), 1.0, 6.0, ((0, 8), (1, 4)), jnp.float32)
    trace_rhs = gaussian(streams_of[1], (N_WIDE, N_NARROW, NB, R, F), 1.0, 6.0, ((0, 8), (1, 4)), jnp.float32)
    block_inverse = draw_block_inverse(jax.random.fold_in(streams_of[14], 71), 0)
    coupling = gaussian(streams_of[3], (N_WIDE, N_NARROW, NB, K, F, F), (8 * F) ** -0.5, 0.1875, ((0, 8), (1, 4)))
    block_neighbours = plant(jax.random.randint(streams_of[4], (N_WIDE, N_NARROW, NB, K), 0, NB + 4 * HB), jax.random.fold_in(streams_of[4], 1), 0, (NB + 4 * HB) - 1).astype(jnp.int32)
    block_send = plant(jax.random.randint(streams_of[5], (N_WIDE, N_NARROW, 4, HB), 0, NB), jax.random.fold_in(streams_of[5], 1), 0, NB - 1).astype(jnp.int32)
    cell_faces = plant(jax.random.randint(streams_of[6], (N_WIDE, N_NARROW, 6, NC), 0, (NB + 4 * HB) * F), jax.random.fold_in(streams_of[6], 1), 0, ((NB + 4 * HB) * F) - 1).astype(jnp.int32)
    face_coeff = jnp.clip(jnp.exp(math.log(2.0) - 2.3025851 * jax.random.uniform(streams_of[7], (N_WIDE, N_NARROW, 6, NC), jnp.float32) ** steps_of(streams_of[7], (N_WIDE, N_NARROW, 6, NC), ((0, 8), (1, 4)), -0.2, 0.2)), 0.2, 2.0)
    cell_source = gaussian(streams_of[8], (N_WIDE, N_NARROW, NC), 1.0, 6.0, ((0, 8), (1, 4)), jnp.float32)
    cell_neighbours = draw_cell_neighbours(jax.random.fold_in(streams_of[14], 71), 0)
    upwind_flags = plant((jax.random.randint(streams_of[10], (N_WIDE, N_NARROW, 6, NC), 0, 2) < 1).astype(jnp.int32), jax.random.fold_in(streams_of[10], 1), 0, 1)
    cell_send = plant(jax.random.randint(streams_of[11], (N_WIDE, N_NARROW, 4, HC), 0, NC), jax.random.fold_in(streams_of[11], 1), 0, NC - 1).astype(jnp.int32)
    saturation = gaussian(streams_of[12], (N_WIDE, N_NARROW, 4, NC), 0.5, 3.0, ((0, 8), (1, 4)), jnp.float32)
    step_ratio = jnp.clip(jnp.exp(math.log(0.2) - 1.3862944 * jax.random.uniform(streams_of[13], (N_WIDE, N_NARROW, NC), jnp.float32) ** steps_of(streams_of[13], (N_WIDE, N_NARROW, NC), ((0, 8), (1, 4)), -0.2, 0.2)), 0.05, 0.2)
    return dict(trace_guess=trace_guess, trace_rhs=trace_rhs, block_inverse=block_inverse, coupling=coupling, block_neighbours=block_neighbours, block_send=block_send, cell_faces=cell_faces, face_coeff=face_coeff, cell_source=cell_source, cell_neighbours=cell_neighbours, upwind_flags=upwind_flags, cell_send=cell_send, saturation=saturation, step_ratio=step_ratio)


def receive(send_data):
    zero_wide = jnp.zeros_like(send_data[:1, :, 0])
    west = jnp.concatenate([zero_wide, send_data[:-1, :, 1]], 0)
    east = jnp.concatenate([send_data[1:, :, 0], zero_wide], 0)
    zero_narrow = jnp.zeros_like(send_data[:, :1, 2])
    south = jnp.concatenate([zero_narrow, send_data[:, :-1, 3]], 1)
    north = jnp.concatenate([send_data[:, 1:, 2], zero_narrow], 1)
    return jnp.stack([west, east, south, north], 2)


def picked(values, index):
    return jax.vmap(jax.vmap(lambda x, i: x[i]))(values, index)


def smooth(extended, inverse, couple, links, rhs):
    near = extended[links]
    coupled = jnp.einsum("bkij,bkrj->bri", couple.astype(jnp.float32), near.astype(jnp.float32))
    resid = (rhs - coupled).astype(jnp.bfloat16)
    return jnp.einsum("bij,brj->bri", inverse.astype(jnp.float32), resid.astype(jnp.float32))


def smooth_slice(items):
    return jax.vmap(smooth)(*items)


def reference(trace_guess, trace_rhs, block_inverse, coupling, block_neighbours, block_send, cell_faces, face_coeff, cell_source, cell_neighbours, upwind_flags, cell_send, saturation, step_ratio):
    n_wide, n_narrow = trace_guess.shape[0], trace_guess.shape[1]
    sends = block_send.reshape(n_wide, n_narrow, 4 * HB)
    current = trace_guess.astype(jnp.bfloat16)
    fresh = trace_guess
    for sweep in range(2):
        outgoing = picked(current, sends).reshape(n_wide, n_narrow, 4, HB, R, F)
        arrived = receive(outgoing).reshape(n_wide, n_narrow, 4 * HB, R, F)
        extended = jnp.concatenate([current, arrived], 2)
        fresh = lax.map(smooth_slice, (extended, block_inverse, coupling, block_neighbours, trace_rhs))
        current = fresh.astype(jnp.bfloat16)
    first_column = current[:, :, :, 0, :]
    outgoing = picked(first_column, sends).reshape(n_wide, n_narrow, 4, HB * F)
    arrived = receive(outgoing).reshape(n_wide, n_narrow, 4 * HB * F)
    face_values = jnp.concatenate([first_column.reshape(n_wide, n_narrow, NB * F), arrived], 2).astype(jnp.float32)
    face_trace = picked(face_values, cell_faces)
    total = jnp.sum(face_coeff, 2)
    pressure = (cell_source + jnp.sum(face_coeff * face_trace, 2)) / total
    flux = face_coeff * (pressure[:, :, None, :] - face_trace)
    cell_out = jax.vmap(jax.vmap(lambda s, c: jnp.transpose(s[:, c], (1, 0, 2))))(saturation, cell_send)
    cell_in = receive(cell_out)
    cell_in = jnp.transpose(cell_in, (0, 1, 3, 2, 4)).reshape(n_wide, n_narrow, 4, 4 * HC)
    ext_sat = jnp.concatenate([saturation, cell_in], 3)
    across_modes = jax.vmap(jax.vmap(lambda e, idx: e[:, idx]))(ext_sat, cell_neighbours)
    flows = []
    for face in range(6):
        axis_mode = face // 2 + 1
        sign = -1.0 if face % 2 == 0 else 1.0
        own = saturation[:, :, 0] + sign * saturation[:, :, axis_mode]
        across = across_modes[:, :, 0, face] - sign * across_modes[:, :, axis_mode, face]
        upwind = jnp.where(upwind_flags[:, :, face] == 1, own, across)
        flows.append(flux[:, :, face] * upwind)
    flow = jnp.stack(flows, 2)
    modes = [saturation[:, :, 0] - step_ratio * jnp.sum(flow, 2)]
    for axis_mode in range(1, 4):
        low, high = 2 * axis_mode - 2, 2 * axis_mode - 1
        volume = 0.5 * (flux[:, :, high] - flux[:, :, low]) * saturation[:, :, 0]
        modes.append(saturation[:, :, axis_mode] + 3.0 * step_ratio * (volume - (flow[:, :, high] - flow[:, :, low])))
    return fresh, jnp.stack(modes, 2)
```

```python
import functools

import jax
import jax.numpy as jnp
from jax import lax
from jax.experimental import pallas as pl
from jax.experimental.pallas import tpu as pltpu
from jax.sharding import PartitionSpec as P

lane_width = 128
tail_rows = 16
vmem_bytes = 48 * 1024 * 1024
axes = ("wide", "narrow")


def pairings(wide, narrow):
    def number(i, j):
        return i * narrow + j

    def close(pairs, partner_of):
        taken = {d for pair in pairs for d in pair}
        for i in range(wide):
            for j in range(narrow):
                partner = partner_of(i, j)
                if number(i, j) in taken:
                    continue
                if 0 <= partner[0] < wide and 0 <= partner[1] < narrow:
                    if number(*partner) not in taken:
                        pairs.append((number(i, j), number(*partner)))
                        taken |= {number(i, j), number(*partner)}
        moves = [(a, b) for a, b in pairs] + [(b, a) for a, b in pairs if a != b]
        sources = {a for a, _ in moves}
        return moves + [(d, d) for d in range(wide * narrow) if d not in sources]

    plans = []
    for first in (0, 1):
        pairs = [
            (number(i, j), number(i + 1, j))
            for i in range(first, wide - 1, 2)
            for j in range(narrow)
        ]
        plans.append(close(pairs, lambda i, j: (i, j ^ 1)))
    for first in (0, 1):
        pairs = [
            (number(i, j), number(i, j + 1))
            for i in range(wide)
            for j in range(first, narrow - 1, 2)
        ]
        plans.append(close(pairs, lambda i, j: (i, narrow - 1 - j)))
    return plans


def trade(pieces, plans):
    return [lax.ppermute(piece, axes, plan) for piece, plan in zip(pieces, plans)]


def sides_of(wide, narrow):
    found = []
    for base, axis, count in ((0, "wide", wide), (2, "narrow", narrow)):
        here = lax.axis_index(axis)
        for first in (0, 1):
            partner = ((here + first) ^ 1) - first
            side = base + jnp.where(partner > here, 1, 0)
            found.append((side, (partner >= 0) & (partner < count)))
    return found


def spread(row):
    return jnp.broadcast_to(row, (8, lane_width))


def take_lanes(row, low):
    return jnp.take_along_axis(row, low, axis=1, mode="promise_in_bounds")


def pack_kernel(mesh_dims, sends, guess, cell_list, sat, out0, out1, out2, out3, picked):
    places = sides_of(*mesh_dims)
    blocks_sent = sends.shape[0]
    size = guess.shape[1]
    groups = sat.shape[0] // 4
    lists = cell_list.shape[0]
    halves = lists // 4
    index = cell_list[...]
    high = index >> 7
    low = index & (lane_width - 1)
    found = jnp.zeros(index.shape, jnp.float32)
    for group in range(groups):
        modes = sat[pl.ds(group * 4, 4), :]
        mean, along_x, along_y = modes[0:1], modes[1:2], modes[2:3]
        four = jnp.concatenate([mean - along_x, mean + along_x, mean - along_y, mean + along_y], 0)
        rows = jnp.concatenate([four] * halves, 0)
        found = jnp.where(high == group, take_lanes(rows, low), found)
    picked[...] = found
    for (side, _), out in zip(places, (out0, out1, out2, out3)):
        for block in range(blocks_sent):
            out[pl.ds(block * size, size), :] = guess[sends[block, side]].astype(jnp.bfloat16)
        values = [picked[pl.ds(half * 4 + side, 1), :] for half in range(halves)]
        coarse = [value.astype(jnp.bfloat16).astype(jnp.float32) for value in values]
        fine = [value - rounded for value, rounded in zip(values, coarse)]
        blank = jnp.zeros((tail_rows - 2 * halves, lane_width), jnp.float32)
        out[pl.ds(blocks_sent * size, tail_rows), :] = jnp.concatenate(
            coarse + fine + [blank], 0
        ).astype(jnp.bfloat16)


def product(left, right):
    return lax.dot_general(
        left, right, (((1,), (1,)), ((), ())), preferred_element_type=jnp.float32
    )


def land(extended, places, arrived, own_count, blocks_sent, size):
    for (side, exists), came in zip(places, arrived):
        for block in range(blocks_sent):
            value = came[pl.ds(block * size, size), :]
            value = jnp.where(exists, value, jnp.zeros_like(value))
            extended[own_count + side * blocks_sent + block] = value


def first_sweep_kernel(
    mesh_dims, links, sends, guess, in0, in1, in2, in3, couple, inverse, rhs,
    smoothed, out0, out1, out2, out3, extended,
):
    places = sides_of(*mesh_dims)
    blocks, size = guess.shape[0], guess.shape[1]
    blocks_sent = sends.shape[0]
    for block in range(blocks):
        extended[block] = guess[block].astype(jnp.bfloat16)
    land(extended, places, (in0, in1, in2, in3), blocks, blocks_sent, size)
    for block in range(blocks):
        near = jnp.concatenate([extended[links[0, block]], extended[links[1, block]]], 1)
        matrix = jnp.concatenate([couple[block, 0], couple[block, 1]], 1)
        resid = (rhs[block] - product(near, matrix)).astype(jnp.bfloat16)
        smoothed[block] = product(resid, inverse[block]).astype(jnp.bfloat16)
    for (side, _), out in zip(places, (out0, out1, out2, out3)):
        for block in range(blocks_sent):
            out[pl.ds(block * size, size), :] = smoothed[sends[block, side]]


def first_column_kernel(
    mesh_dims, links, sends, current, in0, in1, in2, in3, couple, inverse, rhs,
    column, out0, out1, out2, out3, extended,
):
    places = sides_of(*mesh_dims)
    blocks = current.shape[0]
    size = current.shape[1]
    blocks_sent = sends.shape[0]
    for block in range(blocks):
        extended[block] = current[block, 0:tail_rows, :]
    for (side, exists), came in zip(places, (in0, in1, in2, in3)):
        for block in range(blocks_sent):
            value = came[pl.ds(block * size, tail_rows), :]
            value = jnp.where(exists, value, jnp.zeros_like(value))
            extended[blocks + side * blocks_sent + block] = value
    for block in range(blocks):
        near = jnp.concatenate([extended[links[0, block]], extended[links[1, block]]], 1)
        matrix = jnp.concatenate([couple[block, 0], couple[block, 1]], 1)
        resid = (rhs[block, 0:tail_rows, :] - product(near, matrix)).astype(jnp.bfloat16)
        fresh = product(resid, inverse[block])[0:1, :]
        column[pl.ds(block, 1), :] = fresh.astype(jnp.bfloat16).astype(jnp.float32)
    for (side, _), out in zip(places, (out0, out1, out2, out3)):
        rows = [column[pl.ds(sends[block, side], 1), :] for block in range(blocks_sent)]
        blank = jnp.zeros((tail_rows - blocks_sent, lane_width), jnp.float32)
        out[...] = jnp.concatenate(rows + [blank], 0).astype(jnp.bfloat16)


def second_sweep_kernel(
    mesh_dims, links, current, in0, in1, in2, in3, couple, inverse, rhs, fresh, extended,
):
    places = sides_of(*mesh_dims)
    blocks, size = current.shape[0], current.shape[1]
    blocks_sent = in0.shape[0] // size
    for block in range(blocks):
        extended[block] = current[block]
    land(extended, places, (in0, in1, in2, in3), blocks, blocks_sent, size)
    for block in range(blocks):
        near = jnp.concatenate([extended[links[0, block]], extended[links[1, block]]], 1)
        matrix = jnp.concatenate([couple[block, 0], couple[block, 1]], 1)
        resid = (rhs[block] - product(near, matrix)).astype(jnp.bfloat16)
        fresh[block] = product(resid, inverse[block])


def cells_kernel(
    mesh_dims, blocks_sent, halves, column, in0, in1, in2, in3, tail0, tail1, tail2, tail3,
    cell_faces, coeff, source, neighbours, flags, sat, ratio, out, faces, across_rows,
):
    places = sides_of(*mesh_dims)
    own_rows = column.shape[0]
    face_rows = own_rows + 4 * blocks_sent
    groups = sat.shape[0] // 4
    faces[pl.ds(0, own_rows), :] = column[...]
    for (side, exists), came in zip(places, (in0, in1, in2, in3)):
        value = came[...].astype(jnp.float32)[0:blocks_sent]
        value = jnp.where(exists, value, jnp.zeros_like(value))
        for block in range(blocks_sent):
            faces[pl.ds(own_rows + side * blocks_sent + block, 1), :] = value[block : block + 1]
    modes = [sat[pl.ds(mode, groups, stride=4), :] for mode in range(4)]
    stride = across_rows.shape[0] // 6
    for (side, exists), came in zip(places, (tail0, tail1, tail2, tail3)):
        value = came[...].astype(jnp.float32)
        value = value[0:halves] + value[halves : 2 * halves]
        value = jnp.where(exists, value, jnp.zeros_like(value))
        for half in range(halves):
            across_rows[pl.ds(side * stride + groups + half, 1), :] = value[half : half + 1]
    for face in range(6):
        mode = modes[face // 2 + 1]
        across_rows[pl.ds(face * stride, groups), :] = (
            modes[0] + mode if face % 2 == 0 else modes[0] - mode
        )
    weights = [coeff[pl.ds(face * groups, groups), :] for face in range(6)]
    traces = []
    across = []
    for face in range(6):
        parts = []
        for start in range(0, groups, 8):
            index = cell_faces[pl.ds(face * groups + start, 8), :]
            high, low = index >> 7, index & (lane_width - 1)
            value = jnp.zeros((8, lane_width), jnp.float32)
            for row in range(face_rows):
                got = take_lanes(spread(faces[pl.ds(row, 1), :]), low)
                value = jnp.where(high == row, got, value)
            parts.append(value)
        traces.append(jnp.concatenate(parts, 0))
        parts = []
        for start in range(0, groups, 8):
            index = neighbours[pl.ds(face * groups + start, 8), :]
            high, low = index >> 7, index & (lane_width - 1)
            if 0 < face < 4:
                high = jnp.where(high >= groups, high - face * halves, high)
            value = jnp.zeros((8, lane_width), jnp.float32)
            for row in range(groups + halves if face < 4 else groups):
                got = take_lanes(spread(across_rows[pl.ds(face * stride + row, 1), :]), low)
                value = jnp.where(high == row, got, value)
            parts.append(value)
        across.append(jnp.concatenate(parts, 0))
    total = weights[0]
    gained = source[...] + weights[0] * traces[0]
    for face in range(1, 6):
        total = total + weights[face]
        gained = gained + weights[face] * traces[face]
    pressure = gained / total
    flux = [weights[face] * (pressure - traces[face]) for face in range(6)]
    flow = []
    for face in range(6):
        mode = modes[face // 2 + 1]
        own = modes[0] - mode if face % 2 == 0 else modes[0] + mode
        upwind = flags[pl.ds(face * groups, groups), :] == 1
        flow.append(flux[face] * jnp.where(upwind, own, across[face]))
    step = ratio[...]
    out[pl.ds(0, groups, stride=4), :] = modes[0] - step * (
        flow[0] + flow[1] + flow[2] + flow[3] + flow[4] + flow[5]
    )
    for mode in range(1, 4):
        lo, hi = 2 * mode - 2, 2 * mode - 1
        volume = 0.5 * (flux[hi] - flux[lo]) * modes[0]
        out[pl.ds(mode, groups, stride=4), :] = modes[mode] + 3.0 * step * (
            volume - (flow[hi] - flow[lo])
        )


def call(kernel, outs, specs, scratch=(), flops=0, traffic=0):
    return pl.pallas_call(
        kernel,
        out_shape=outs,
        in_specs=specs,
        out_specs=jax.tree.map(lambda _: pl.BlockSpec(memory_space=pltpu.VMEM), outs),
        scratch_shapes=list(scratch),
        compiler_params=pltpu.CompilerParams(vmem_limit_bytes=vmem_bytes),
        cost_estimate=pl.CostEstimate(flops=flops, bytes_accessed=traffic, transcendentals=0),
    )


scalars = pl.BlockSpec(memory_space=pltpu.SMEM)
whole = pl.BlockSpec(memory_space=pltpu.VMEM)


def by_cells(array):
    return array.reshape(-1, lane_width)


def by_groups(array):
    rows = array.shape[0]
    return jnp.swapaxes(array.reshape(rows, -1, lane_width), 0, 1).reshape(-1, lane_width)


def per_device(
    mesh_dims,
    plans,
    trace_guess,
    trace_rhs,
    block_inverse,
    coupling,
    block_neighbours,
    block_send,
    cell_faces,
    face_coeff,
    cell_source,
    cell_neighbours,
    upwind_flags,
    cell_send,
    saturation,
    step_ratio,
):
    guess = trace_guess[0, 0]
    rhs = trace_rhs[0, 0]
    inverse = block_inverse[0, 0]
    couple = coupling[0, 0]
    links = block_neighbours[0, 0].T
    sends = block_send[0, 0].T
    blocks, columns, size = guess.shape
    blocks_sent = sends.shape[0]
    halo_rows = blocks_sent * columns
    extended_blocks = blocks + 4 * blocks_sent
    sat = by_groups(saturation[0, 0])
    cell_list = by_groups(cell_send[0, 0])
    halves = cell_list.shape[0] // 4
    groups = sat.shape[0] // 4
    half, single = jnp.bfloat16, jnp.float32

    packed = call(
        functools.partial(pack_kernel, mesh_dims),
        [jax.ShapeDtypeStruct((halo_rows + tail_rows, size), half)] * 4,
        [scalars, whole, whole, whole],
        [pltpu.VMEM((4 * halves, lane_width), single)],
    )(sends, guess, cell_list, sat)
    arrived = trade(packed, plans)

    sweep_flops = 6 * blocks * columns * size * size
    smoothed, *packed = call(
        functools.partial(first_sweep_kernel, mesh_dims),
        [jax.ShapeDtypeStruct(guess.shape, half)]
        + [jax.ShapeDtypeStruct((halo_rows, size), half)] * 4,
        [scalars, scalars] + [whole] * 8,
        [pltpu.VMEM((extended_blocks, columns, size), half)],
        sweep_flops,
    )(links, sends, guess, *arrived, couple, inverse, rhs)
    swept = trade(packed, plans)

    column, *packed = call(
        functools.partial(first_column_kernel, mesh_dims),
        [jax.ShapeDtypeStruct((blocks, size), single)]
        + [jax.ShapeDtypeStruct((tail_rows, size), half)] * 4,
        [scalars, scalars] + [whole] * 8,
        [pltpu.VMEM((extended_blocks, tail_rows, size), half)],
        sweep_flops // 8,
    )(links, sends, smoothed, *swept, couple, inverse, rhs)
    edges = trade(packed, plans)

    traces = call(
        functools.partial(second_sweep_kernel, mesh_dims),
        jax.ShapeDtypeStruct(guess.shape, single),
        [scalars] + [whole] * 8,
        [pltpu.VMEM((extended_blocks, columns, size), half)],
        sweep_flops,
    )(links, smoothed, *swept, couple, inverse, rhs)

    tails = [piece[halo_rows:] for piece in arrived]
    face_rows = -(-extended_blocks // 8) * 8
    cell_rows = -(-(groups + halves) // 8) * 8
    following = call(
        functools.partial(cells_kernel, mesh_dims, blocks_sent, halves),
        jax.ShapeDtypeStruct(sat.shape, single),
        [whole] * 16,
        [
            pltpu.VMEM((face_rows, lane_width), single),
            pltpu.VMEM((6 * cell_rows, lane_width), single),
        ],
    )(
        column,
        *edges,
        *tails,
        by_cells(cell_faces[0, 0]),
        by_cells(face_coeff[0, 0]),
        by_cells(cell_source[0]),
        by_cells(cell_neighbours[0, 0]),
        by_cells(upwind_flags[0, 0]),
        sat,
        by_cells(step_ratio[0]),
    )
    saturation_next = jnp.swapaxes(following.reshape(groups, 4, lane_width), 0, 1).reshape(4, -1)
    return traces[None, None], saturation_next[None, None]


def solution(mesh):
    mesh_dims = (mesh.shape["wide"], mesh.shape["narrow"])

    def spec(rank):
        return P("wide", "narrow", *([None] * (rank - 2)))

    placed = tuple(spec(rank) for rank in (5, 5, 5, 6, 4, 4, 4, 4, 3, 4, 4, 4, 4, 3))
    return jax.shard_map(
        functools.partial(per_device, mesh_dims, pairings(*mesh_dims)),
        mesh=mesh,
        in_specs=placed,
        out_specs=(spec(5), spec(4)),
        check_vma=False,
    )
```

```python
import functools

import jax
import jax.numpy as jnp
from jax import lax
from jax.experimental import pallas as pl
from jax.experimental.pallas import tpu as pltpu
from jax.sharding import PartitionSpec as P

lane_width = 128
tail_rows = 16
vmem_bytes = 24 * 1024 * 1024
axes = ("wide", "narrow")


def pairings(wide, narrow):
    def number(i, j):
        return i * narrow + j

    def close(pairs, partner_of):
        taken = {d for pair in pairs for d in pair}
        for i in range(wide):
            for j in range(narrow):
                partner = partner_of(i, j)
                if number(i, j) in taken:
                    continue
                if 0 <= partner[0] < wide and 0 <= partner[1] < narrow:
                    if number(*partner) not in taken:
                        pairs.append((number(i, j), number(*partner)))
                        taken |= {number(i, j), number(*partner)}
        moves = [(a, b) for a, b in pairs] + [(b, a) for a, b in pairs if a != b]
        sources = {a for a, _ in moves}
        return moves + [(d, d) for d in range(wide * narrow) if d not in sources]

    plans = []
    for first in (0, 1):
        pairs = [
            (number(i, j), number(i + 1, j))
            for i in range(first, wide - 1, 2)
            for j in range(narrow)
        ]
        plans.append(close(pairs, lambda i, j: (i, j ^ 1)))
    for first in (0, 1):
        pairs = [
            (number(i, j), number(i, j + 1))
            for i in range(wide)
            for j in range(first, narrow - 1, 2)
        ]
        plans.append(close(pairs, lambda i, j: (i, narrow - 1 - j)))
    return plans


def trade(pieces, plans):
    return [lax.ppermute(piece, axes, plan) for piece, plan in zip(pieces, plans)]


def sides_of(wide, narrow):
    found = []
    for base, axis, count in ((0, "wide", wide), (2, "narrow", narrow)):
        here = lax.axis_index(axis)
        for first in (0, 1):
            partner = ((here + first) ^ 1) - first
            side = base + jnp.where(partner > here, 1, 0)
            found.append((side, (partner >= 0) & (partner < count)))
    return found


def spread(row):
    return jnp.broadcast_to(row, (8, lane_width))


def take_lanes(row, low):
    return jnp.take_along_axis(row, low, axis=1, mode="promise_in_bounds")


def pack_kernel(
    mesh_dims, sends_far, guess_far, list_far, sat_far,
    out0, out1, out2, out3, rounded,
    sends, guess, cell_list, sat, picked, arrivals,
):
    places = sides_of(*mesh_dims)
    blocks, size = guess.shape[0], guess.shape[1]
    copies = [
        pltpu.make_async_copy(far, near, arrivals.at[slot])
        for slot, (far, near) in enumerate(
            ((list_far, cell_list), (sat_far, sat), (sends_far, sends))
        )
    ]
    loads = [
        pltpu.make_async_copy(guess_far.at[block], guess.at[block], arrivals.at[3 + block])
        for block in range(blocks)
    ]
    for copy in copies + loads:
        copy.start()
    copies[0].wait()
    copies[1].wait()
    blocks_sent = sends.shape[0]
    groups = sat.shape[0] // 4
    lists = cell_list.shape[0]
    halves = lists // 4
    index = cell_list[...]
    high = index >> 7
    low = index & (lane_width - 1)
    found = jnp.zeros(index.shape, jnp.float32)
    for group in range(groups):
        modes = sat[pl.ds(group * 4, 4), :]
        mean, along_x, along_y = modes[0:1], modes[1:2], modes[2:3]
        four = jnp.concatenate([mean - along_x, mean + along_x, mean - along_y, mean + along_y], 0)
        rows = jnp.concatenate([four] * halves, 0)
        found = jnp.where(high == group, take_lanes(rows, low), found)
    picked[...] = found
    for (side, _), out in zip(places, (out0, out1, out2, out3)):
        values = [picked[pl.ds(half * 4 + side, 1), :] for half in range(halves)]
        coarse = [value.astype(jnp.bfloat16).astype(jnp.float32) for value in values]
        fine = [value - rounded_value for value, rounded_value in zip(values, coarse)]
        blank = jnp.zeros((tail_rows - 2 * halves, lane_width), jnp.float32)
        out[pl.ds(blocks_sent * size, tail_rows), :] = jnp.concatenate(
            coarse + fine + [blank], 0
        ).astype(jnp.bfloat16)
    for block in range(blocks):
        loads[block].wait()
        rounded[block] = guess[block].astype(jnp.bfloat16)
    copies[2].wait()
    for (side, _), out in zip(places, (out0, out1, out2, out3)):
        for block in range(blocks_sent):
            out[pl.ds(block * size, size), :] = rounded[sends[block, side]]


def fetch_kernel(count, *refs):
    fars, nears, arrivals = refs[1 : 1 + count], refs[1 + count : 1 + 2 * count], refs[-1]
    copies = [
        pltpu.make_async_copy(far, near, arrivals.at[slot])
        for slot, (far, near) in enumerate(zip(fars, nears))
    ]
    for copy in copies:
        copy.start()
    for copy in copies:
        copy.wait()


def product(left, right):
    return lax.dot_general(
        left, right, (((1,), (1,)), ((), ())), preferred_element_type=jnp.float32
    )


def relax(extended, links, couple, inverse, rhs, block):
    near = jnp.concatenate([extended[links[0, block]], extended[links[1, block]]], 1)
    matrix = jnp.concatenate([couple[block, 0], couple[block, 1]], 1)
    resid = (rhs[block, 0 : near.shape[0], :] - product(near, matrix)).astype(jnp.bfloat16)
    return product(resid, inverse[block])


def extend(extended, own, places, arrived, blocks_sent, size):
    rows = extended.shape[1]
    own_count = own.shape[0]
    for block in range(own_count):
        extended[block] = own[block, 0:rows, :]
    for (side, exists), came in zip(places, arrived):
        for block in range(blocks_sent):
            value = came[pl.ds(block * size, rows), :]
            value = jnp.where(exists, value, jnp.zeros_like(value))
            extended[own_count + side * blocks_sent + block] = value


def first_edge_kernel(
    mesh_dims, links, sends, own, in0, in1, in2, in3, couple, inverse, rhs,
    extended, out0, out1, out2, out3,
):
    places = sides_of(*mesh_dims)
    size = own.shape[1]
    blocks_sent = sends.shape[0]
    extend(extended, own, places, (in0, in1, in2, in3), blocks_sent, size)
    for (side, _), out in zip(places, (out0, out1, out2, out3)):
        for block in range(blocks_sent):
            fresh = relax(extended, links, couple, inverse, rhs, sends[block, side])
            out[pl.ds(block * size, size), :] = fresh.astype(jnp.bfloat16)


def look_up(table, first_row, rows, high, low):
    value = jnp.zeros((8, lane_width), jnp.float32)
    for row in range(rows):
        got = take_lanes(spread(table[pl.ds(first_row + row, 1), :]), low)
        value = jnp.where(high == row, got, value)
    return value


def first_sweep_kernel(
    mesh_dims, halves, links, extended, couple, inverse, rhs,
    sat, neighbours, tail0, tail1, tail2, tail3,
    smoothed, across, across_rows,
):
    places = sides_of(*mesh_dims)
    groups = sat.shape[0] // 4
    stride = across_rows.shape[0] // 6
    modes = [sat[pl.ds(mode, groups, stride=4), :] for mode in range(4)]
    for (side, exists), came in zip(places, (tail0, tail1, tail2, tail3)):
        value = came[...].astype(jnp.float32)
        value = value[0:halves] + value[halves : 2 * halves]
        value = jnp.where(exists, value, jnp.zeros_like(value))
        for half in range(halves):
            across_rows[pl.ds(side * stride + groups + half, 1), :] = value[half : half + 1]
    for face in range(6):
        mode = modes[face // 2 + 1]
        across_rows[pl.ds(face * stride, groups), :] = (
            modes[0] + mode if face % 2 == 0 else modes[0] - mode
        )
    for block in range(smoothed.shape[0]):
        smoothed[block] = relax(extended, links, couple, inverse, rhs, block).astype(jnp.bfloat16)
    for face in range(6):
        for start in range(0, groups, 8):
            index = neighbours[pl.ds(face * groups + start, 8), :]
            high, low = index >> 7, index & (lane_width - 1)
            if 0 < face < 4:
                high = jnp.where(high >= groups, high - face * halves, high)
            rows = groups + halves if face < 4 else groups
            across[pl.ds(face * groups + start, 8), :] = look_up(
                across_rows, face * stride, rows, high, low
            )


def second_edge_kernel(
    mesh_dims, links, sends, own, in0, in1, in2, in3, couple, inverse, rhs,
    out0, out1, out2, out3, extended,
):
    places = sides_of(*mesh_dims)
    size = own.shape[1]
    blocks_sent = sends.shape[0]
    extend(extended, own, places, (in0, in1, in2, in3), blocks_sent, size)
    for (side, _), out in zip(places, (out0, out1, out2, out3)):
        rows = [
            relax(extended, links, couple, inverse, rhs, sends[block, side])[0:1, :]
            for block in range(blocks_sent)
        ]
        blank = jnp.zeros((tail_rows - blocks_sent, lane_width), jnp.float32)
        out[...] = jnp.concatenate(rows + [blank], 0).astype(jnp.bfloat16)


def second_sweep_kernel(
    mesh_dims, links, own, in0, in1, in2, in3, couple, inverse, rhs,
    traces, column, extended, fresh, departures,
):
    places = sides_of(*mesh_dims)
    blocks, size = own.shape[0], own.shape[1]
    blocks_sent = in0.shape[0] // size
    extend(extended, own, places, (in0, in1, in2, in3), blocks_sent, size)
    stores = []
    for block in range(blocks):
        value = relax(extended, links, couple, inverse, rhs, block)
        fresh[block] = value
        stores.append(
            pltpu.make_async_copy(fresh.at[block], traces.at[block], departures.at[block])
        )
        stores[block].start()
        column[pl.ds(block, 1), :] = value[0:1].astype(jnp.bfloat16).astype(jnp.float32)
    for store in stores:
        store.wait()


def cells_kernel(
    mesh_dims, blocks_sent, column, in0, in1, in2, in3, across,
    cell_faces, coeff, source, flags, sat, ratio, out, faces,
):
    places = sides_of(*mesh_dims)
    own_rows = column.shape[0]
    face_rows = own_rows + 4 * blocks_sent
    groups = sat.shape[0] // 4
    faces[pl.ds(0, own_rows), :] = column[...]
    for (side, exists), came in zip(places, (in0, in1, in2, in3)):
        value = came[...].astype(jnp.float32)[0:blocks_sent]
        value = jnp.where(exists, value, jnp.zeros_like(value))
        for block in range(blocks_sent):
            faces[pl.ds(own_rows + side * blocks_sent + block, 1), :] = value[block : block + 1]
    modes = [sat[pl.ds(mode, groups, stride=4), :] for mode in range(4)]
    weights = [coeff[pl.ds(face * groups, groups), :] for face in range(6)]
    traces = []
    for face in range(6):
        parts = []
        for start in range(0, groups, 8):
            index = cell_faces[pl.ds(face * groups + start, 8), :]
            parts.append(look_up(faces, 0, face_rows, index >> 7, index & (lane_width - 1)))
        traces.append(jnp.concatenate(parts, 0))
    total = weights[0]
    gained = source[...] + weights[0] * traces[0]
    for face in range(1, 6):
        total = total + weights[face]
        gained = gained + weights[face] * traces[face]
    pressure = gained / total
    flux = [weights[face] * (pressure - traces[face]) for face in range(6)]
    flow = []
    for face in range(6):
        mode = modes[face // 2 + 1]
        own = modes[0] - mode if face % 2 == 0 else modes[0] + mode
        rows = pl.ds(face * groups, groups)
        flow.append(flux[face] * jnp.where(flags[rows, :] == 1, own, across[rows, :]))
    step = ratio[...]
    out[pl.ds(0, groups, stride=4), :] = modes[0] - step * (
        flow[0] + flow[1] + flow[2] + flow[3] + flow[4] + flow[5]
    )
    for mode in range(1, 4):
        lo, hi = 2 * mode - 2, 2 * mode - 1
        volume = 0.5 * (flux[hi] - flux[lo]) * modes[0]
        out[pl.ds(mode, groups, stride=4), :] = modes[mode] + 3.0 * step * (
            volume - (flow[hi] - flow[lo])
        )


scalars = pl.BlockSpec(memory_space=pltpu.SMEM)
whole = pl.BlockSpec(memory_space=pltpu.VMEM)
far = pl.BlockSpec(memory_space=pl.ANY)


def call(kernel, outs, specs, scratch=(), flops=0, traffic=0, out_specs=None):
    return pl.pallas_call(
        kernel,
        out_shape=outs,
        in_specs=specs,
        out_specs=[whole] * len(outs) if out_specs is None else out_specs,
        scratch_shapes=list(scratch),
        compiler_params=pltpu.CompilerParams(vmem_limit_bytes=vmem_bytes),
        cost_estimate=pl.CostEstimate(flops=flops, bytes_accessed=traffic, transcendentals=0),
    )


def keep_far(array):
    return pltpu.with_memory_space_constraint(array, pltpu.HBM)


def by_cells(array):
    return array.reshape(-1, lane_width)


def by_groups(array):
    rows = array.shape[0]
    return jnp.swapaxes(array.reshape(rows, -1, lane_width), 0, 1).reshape(-1, lane_width)


def per_device(
    mesh_dims,
    plans,
    trace_guess,
    trace_rhs,
    block_inverse,
    coupling,
    block_neighbours,
    block_send,
    cell_faces,
    face_coeff,
    cell_source,
    cell_neighbours,
    upwind_flags,
    cell_send,
    saturation,
    step_ratio,
):
    guess = trace_guess[0, 0]
    rhs = trace_rhs[0, 0]
    inverse = block_inverse[0, 0]
    couple = coupling[0, 0]
    links = block_neighbours[0, 0].T
    sends = block_send[0, 0].T
    blocks, columns, size = guess.shape
    blocks_sent = sends.shape[0]
    halo_rows = blocks_sent * columns
    extended_blocks = blocks + 4 * blocks_sent
    sat = by_groups(saturation[0, 0])
    cell_list = by_groups(cell_send[0, 0])
    halves = cell_list.shape[0] // 4
    groups = sat.shape[0] // 4
    half, single = jnp.bfloat16, jnp.float32

    def like(array):
        return jax.ShapeDtypeStruct(array.shape, array.dtype)

    *packed, own = call(
        functools.partial(pack_kernel, mesh_dims),
        [jax.ShapeDtypeStruct((halo_rows + tail_rows, size), half)] * 4
        + [jax.ShapeDtypeStruct(guess.shape, half)],
        [far] * 4,
        [
            pltpu.SMEM(sends.shape, jnp.int32),
            pltpu.VMEM(guess.shape, single),
            pltpu.VMEM(cell_list.shape, jnp.int32),
            pltpu.VMEM(sat.shape, single),
            pltpu.VMEM((4 * halves, lane_width), single),
            pltpu.SemaphoreType.DMA((3 + blocks,)),
        ],
    )(*map(keep_far, (sends, guess, cell_list, sat)))
    arrived = trade(packed, plans)

    remote = [
        couple,
        inverse,
        rhs,
        by_cells(cell_faces[0, 0]),
        by_cells(face_coeff[0, 0]),
        by_cells(cell_source[0]),
        by_cells(cell_neighbours[0, 0]),
        by_cells(upwind_flags[0, 0]),
        sat,
        by_cells(step_ratio[0]),
        links,
        sends,
    ]
    (
        couple,
        inverse,
        rhs,
        cell_faces,
        coeff,
        source,
        neighbours,
        flags,
        sat,
        ratio,
        links,
        sends,
    ) = call(
        functools.partial(fetch_kernel, len(remote)),
        [like(array) for array in remote],
        [far] * (1 + len(remote)),
        [pltpu.SemaphoreType.DMA((len(remote),))],
        traffic=4 * guess.size,
    )(own, *map(keep_far, remote))

    sweep_flops = 6 * blocks * columns * size * size
    extended, *packed = call(
        functools.partial(first_edge_kernel, mesh_dims),
        [jax.ShapeDtypeStruct((extended_blocks, columns, size), half)]
        + [jax.ShapeDtypeStruct((halo_rows, size), half)] * 4,
        [scalars, scalars] + [whole] * 8,
        flops=sweep_flops // 2,
    )(links, sends, own, *arrived, couple, inverse, rhs)
    swept = trade(packed, plans)

    tails = [piece[halo_rows:] for piece in arrived]
    cell_rows = -(-(groups + halves) // 8) * 8
    smoothed, across = call(
        functools.partial(first_sweep_kernel, mesh_dims, halves),
        [like(own), jax.ShapeDtypeStruct(neighbours.shape, single)],
        [scalars] + [whole] * 10,
        [pltpu.VMEM((6 * cell_rows, lane_width), single)],
        sweep_flops,
    )(links, extended, couple, inverse, rhs, sat, neighbours, *tails)

    edges = trade(
        call(
            functools.partial(second_edge_kernel, mesh_dims),
            [jax.ShapeDtypeStruct((tail_rows, size), half)] * 4,
            [scalars, scalars] + [whole] * 8,
            [pltpu.VMEM((extended_blocks, tail_rows, size), half)],
            sweep_flops // 16,
        )(links, sends, smoothed, *swept, couple, inverse, rhs),
        plans,
    )

    traces, column = call(
        functools.partial(second_sweep_kernel, mesh_dims),
        [jax.ShapeDtypeStruct(guess.shape, single), jax.ShapeDtypeStruct((blocks, size), single)],
        [scalars] + [whole] * 8,
        [
            pltpu.VMEM((extended_blocks, columns, size), half),
            pltpu.VMEM(guess.shape, single),
            pltpu.SemaphoreType.DMA((blocks,)),
        ],
        sweep_flops,
        out_specs=[far, whole],
    )(links, smoothed, *swept, couple, inverse, rhs)

    face_rows = -(-extended_blocks // 8) * 8
    (following,) = call(
        functools.partial(cells_kernel, mesh_dims, blocks_sent),
        [like(sat)],
        [whole] * 12,
        [pltpu.VMEM((face_rows, lane_width), single)],
    )(column, *edges, across, cell_faces, coeff, source, flags, sat, ratio)
    saturation_next = jnp.swapaxes(following.reshape(groups, 4, lane_width), 0, 1).reshape(4, -1)
    return traces[None, None], saturation_next[None, None]


def solution(mesh):
    mesh_dims = (mesh.shape["wide"], mesh.shape["narrow"])

    def spec(rank):
        return P("wide", "narrow", *([None] * (rank - 2)))

    placed = tuple(spec(rank) for rank in (5, 5, 5, 6, 4, 4, 4, 4, 3, 4, 4, 4, 4, 3))
    return jax.shard_map(
        functools.partial(per_device, mesh_dims, pairings(*mesh_dims)),
        mesh=mesh,
        in_specs=placed,
        out_specs=(spec(5), spec(4)),
        check_vma=False,
    )
```

```python
import functools

import jax
import jax.numpy as jnp
from jax import lax
from jax.experimental import pallas as pl
from jax.experimental.pallas import tpu as pltpu
from jax.sharding import PartitionSpec as P

lane_width = 128
tail_rows = 16
vmem_bytes = 24 * 1024 * 1024
axes = ("wide", "narrow")


def pairings(wide, narrow):
    def number(i, j):
        return i * narrow + j

    def close(pairs, partner_of):
        taken = {d for pair in pairs for d in pair}
        for i in range(wide):
            for j in range(narrow):
                partner = partner_of(i, j)
                if number(i, j) in taken:
                    continue
                if 0 <= partner[0] < wide and 0 <= partner[1] < narrow:
                    if number(*partner) not in taken:
                        pairs.append((number(i, j), number(*partner)))
                        taken |= {number(i, j), number(*partner)}
        moves = [(a, b) for a, b in pairs] + [(b, a) for a, b in pairs if a != b]
        sources = {a for a, _ in moves}
        return moves + [(d, d) for d in range(wide * narrow) if d not in sources]

    plans = []
    for first in (0, 1):
        pairs = [
            (number(i, j), number(i + 1, j))
            for i in range(first, wide - 1, 2)
            for j in range(narrow)
        ]
        plans.append(close(pairs, lambda i, j: (i, j ^ 1)))
    for first in (0, 1):
        pairs = [
            (number(i, j), number(i, j + 1))
            for i in range(wide)
            for j in range(first, narrow - 1, 2)
        ]
        plans.append(close(pairs, lambda i, j: (i, narrow - 1 - j)))
    return plans


def trade(pieces, plans):
    return [lax.ppermute(piece, axes, plan) for piece, plan in zip(pieces, plans)]


def sides_of(wide, narrow):
    found = []
    for base, axis, count in ((0, "wide", wide), (2, "narrow", narrow)):
        here = lax.axis_index(axis)
        for first in (0, 1):
            partner = ((here + first) ^ 1) - first
            side = base + jnp.where(partner > here, 1, 0)
            found.append((side, (partner >= 0) & (partner < count)))
    return found


def spread(row):
    return jnp.broadcast_to(row, (8, lane_width))


def take_lanes(row, low):
    return jnp.take_along_axis(row, low, axis=1, mode="promise_in_bounds")


def pack_kernel(
    mesh_dims, sends_far, guess_far, list_far, sat_far,
    out0, out1, out2, out3, extended,
    sends, guess, cell_list, sat, picked, arrivals,
):
    places = sides_of(*mesh_dims)
    blocks, size = guess.shape[0], guess.shape[1]
    copies = [
        pltpu.make_async_copy(far, near, arrivals.at[slot])
        for slot, (far, near) in enumerate(
            ((list_far, cell_list), (sat_far, sat), (sends_far, sends))
        )
    ]
    loads = [
        pltpu.make_async_copy(guess_far.at[block], guess.at[block], arrivals.at[3 + block])
        for block in range(blocks)
    ]
    for copy in copies + loads:
        copy.start()
    for copy in copies:
        copy.wait()
    blocks_sent = sends.shape[0]
    groups = sat.shape[0] // 4
    lists = cell_list.shape[0]
    halves = lists // 4
    index = cell_list[...]
    high = index >> 7
    low = index & (lane_width - 1)
    found = jnp.zeros(index.shape, jnp.float32)
    for group in range(groups):
        modes = sat[pl.ds(group * 4, 4), :]
        mean, along_x, along_y = modes[0:1], modes[1:2], modes[2:3]
        four = jnp.concatenate([mean - along_x, mean + along_x, mean - along_y, mean + along_y], 0)
        rows = jnp.concatenate([four] * halves, 0)
        found = jnp.where(high == group, take_lanes(rows, low), found)
    picked[...] = found
    for (side, _), out in zip(places, (out0, out1, out2, out3)):
        values = [picked[pl.ds(half * 4 + side, 1), :] for half in range(halves)]
        coarse = [value.astype(jnp.bfloat16).astype(jnp.float32) for value in values]
        fine = [value - rounded for value, rounded in zip(values, coarse)]
        blank = jnp.zeros((tail_rows - 2 * halves, lane_width), jnp.float32)
        out[pl.ds(blocks_sent * size, tail_rows), :] = jnp.concatenate(
            coarse + fine + [blank], 0
        ).astype(jnp.bfloat16)
    listed = listed_blocks(sends, places)
    for block in range(blocks):
        loads[block].wait()
        extended[block] = guess[block].astype(jnp.bfloat16)
    for picks, out in zip(listed, (out0, out1, out2, out3)):
        for slot, block in enumerate(picks):
            out[pl.ds(slot * size, size), :] = extended[block]


def listed_blocks(sends, places):
    value = sends[...]
    count = value.shape[0]
    sides = [[value[slot, side] for slot in range(count)] for side in range(4)]
    found = []
    for pairing, (side, _) in enumerate(places):
        first = 0 if pairing < 2 else 2
        found.append(
            [jnp.where(side == first, a, b) for a, b in zip(sides[first], sides[first + 1])]
        )
    return found


def linked_blocks(links):
    value = links[...]
    return [[value[k, block] for k in range(2)] for block in range(value.shape[1])]


def fetch_kernel(count, *refs):
    fars, nears, arrivals = refs[1 : 1 + count], refs[1 + count : 1 + 2 * count], refs[-1]
    copies = [
        pltpu.make_async_copy(far, near, arrivals.at[slot])
        for slot, (far, near) in enumerate(zip(fars, nears))
    ]
    for copy in copies:
        copy.start()
    for copy in copies:
        copy.wait()
    links, sends = nears[-2][...], nears[-1][...]
    for k, near in enumerate(refs[1 + 2 * count : -1]):
        chosen = jnp.zeros_like(sends)
        for block in range(links.shape[1]):
            chosen = jnp.where(sends == block, links[k, block], chosen)
        near[...] = chosen


def product(left, right):
    return lax.dot_general(
        left, right, (((1,), (1,)), ((), ())), preferred_element_type=jnp.float32
    )


def relax(extended, links, couple, inverse, rhs, block, rows):
    near = jnp.concatenate([extended[link, 0:rows, :] for link in links], 1)
    matrix = jnp.concatenate([couple[block, k] for k in range(len(links))], 1)
    resid = (rhs[block, 0:rows, :] - product(near, matrix)).astype(jnp.bfloat16)
    return product(resid, inverse[block])


def land(extended, places, arrived, blocks_sent):
    own_count = extended.shape[0] - 4 * blocks_sent
    size = extended.shape[1]
    for (side, exists), came in zip(places, arrived):
        for block in range(blocks_sent):
            value = came[pl.ds(block * size, size), :]
            value = jnp.where(exists, value, jnp.zeros_like(value))
            extended[own_count + side * blocks_sent + block] = value


def first_edge_kernel(
    mesh_dims, sends, near0, near1, _, in0, in1, in2, in3, couple, inverse, rhs,
    extended, out0, out1, out2, out3,
):
    places = sides_of(*mesh_dims)
    size = extended.shape[1]
    listed = listed_blocks(sends, places)
    links = [listed_blocks(near, places) for near in (near0, near1)]
    land(extended, places, (in0, in1, in2, in3), sends.shape[0])
    for pairing, out in enumerate((out0, out1, out2, out3)):
        for slot, block in enumerate(listed[pairing]):
            pair = [links[k][pairing][slot] for k in range(2)]
            fresh = relax(extended, pair, couple, inverse, rhs, block, size)
            out[pl.ds(slot * size, size), :] = fresh.astype(jnp.bfloat16)


def look_up(table, first_row, rows, high, low, value):
    for row in rows:
        got = take_lanes(spread(table[pl.ds(first_row + row, 1), :]), low)
        value = jnp.where(high == row, got, value)
    return value


def nothing():
    return jnp.zeros((8, lane_width), jnp.float32)


def first_sweep_kernel(
    mesh_dims, halves, links, extended, couple, inverse, rhs,
    sat, neighbours, tail0, tail1, tail2, tail3,
    smoothed, across, across_rows,
):
    places = sides_of(*mesh_dims)
    groups = sat.shape[0] // 4
    stride = across_rows.shape[0] // 6
    modes = [sat[pl.ds(mode, groups, stride=4), :] for mode in range(4)]
    for (side, exists), came in zip(places, (tail0, tail1, tail2, tail3)):
        value = came[...].astype(jnp.float32)
        value = value[0:halves] + value[halves : 2 * halves]
        value = jnp.where(exists, value, jnp.zeros_like(value))
        for half in range(halves):
            across_rows[pl.ds(side * stride + groups + half, 1), :] = value[half : half + 1]
    for face in range(6):
        mode = modes[face // 2 + 1]
        across_rows[pl.ds(face * stride, groups), :] = (
            modes[0] + mode if face % 2 == 0 else modes[0] - mode
        )
    for block, pair in enumerate(linked_blocks(links)):
        fresh = relax(extended, pair, couple, inverse, rhs, block, extended.shape[1])
        smoothed[block] = fresh.astype(jnp.bfloat16)
    for face in range(6):
        for start in range(0, groups, 8):
            index = neighbours[pl.ds(face * groups + start, 8), :]
            high, low = index >> 7, index & (lane_width - 1)
            if 0 < face < 4:
                high = jnp.where(high >= groups, high - face * halves, high)
            rows = range(groups + halves if face < 4 else groups)
            across[pl.ds(face * groups + start, 8), :] = look_up(
                across_rows, face * stride, rows, high, low, nothing()
            )


def second_edge_kernel(
    mesh_dims, sends, near0, near1, _, in0, in1, in2, in3, couple, inverse, rhs,
    extended, out0, out1, out2, out3,
):
    places = sides_of(*mesh_dims)
    listed = listed_blocks(sends, places)
    links = [listed_blocks(near, places) for near in (near0, near1)]
    land(extended, places, (in0, in1, in2, in3), sends.shape[0])
    for pairing, out in enumerate((out0, out1, out2, out3)):
        rows = []
        for slot, block in enumerate(listed[pairing]):
            pair = [links[k][pairing][slot] for k in range(2)]
            fresh = relax(extended, pair, couple, inverse, rhs, block, tail_rows)
            rows.append(fresh[0:1, :])
        blank = jnp.zeros((tail_rows - len(rows), lane_width), jnp.float32)
        out[...] = jnp.concatenate(rows + [blank], 0).astype(jnp.bfloat16)


def second_sweep_kernel(
    links, extended, couple, inverse, rhs, cell_faces,
    traces, partial, fresh, column, departures,
):
    stores = []
    for block, pair in enumerate(linked_blocks(links)):
        value = relax(extended, pair, couple, inverse, rhs, block, extended.shape[1])
        fresh[block] = value
        stores.append(
            pltpu.make_async_copy(fresh.at[block], traces.at[block], departures.at[block])
        )
        stores[block].start()
        column[pl.ds(block, 1), :] = value[0:1].astype(jnp.bfloat16).astype(jnp.float32)
    for start in range(0, cell_faces.shape[0], 8):
        index = cell_faces[pl.ds(start, 8), :]
        rows = range(column.shape[0])
        partial[pl.ds(start, 8), :] = look_up(
            column, 0, rows, index >> 7, index & (lane_width - 1), nothing()
        )
    for store in stores:
        store.wait()


def cells_kernel(
    mesh_dims, blocks, blocks_sent, partial, in2, in3, in0, in1, across,
    cell_faces, coeff, source, flags, sat, ratio, out, faces,
):
    places = sides_of(*mesh_dims)
    groups = sat.shape[0] // 4
    for (side, exists), came in zip(places, (in0, in1, in2, in3)):
        value = came[...].astype(jnp.float32)[0:blocks_sent]
        value = jnp.where(exists, value, jnp.zeros_like(value))
        for block in range(blocks_sent):
            faces[pl.ds(side * blocks_sent + block, 1), :] = value[block : block + 1]
    modes = [sat[pl.ds(mode, groups, stride=4), :] for mode in range(4)]
    weights = [coeff[pl.ds(face * groups, groups), :] for face in range(6)]
    traces = []
    for face in range(6):
        parts = []
        for start in range(0, groups, 8):
            rows = pl.ds(face * groups + start, 8)
            index = cell_faces[rows, :]
            high, low = (index >> 7) - blocks, index & (lane_width - 1)
            parts.append(look_up(faces, 0, range(4 * blocks_sent), high, low, partial[rows, :]))
        traces.append(jnp.concatenate(parts, 0))
    total = weights[0]
    gained = source[...] + weights[0] * traces[0]
    for face in range(1, 6):
        total = total + weights[face]
        gained = gained + weights[face] * traces[face]
    pressure = gained / total
    flux = [weights[face] * (pressure - traces[face]) for face in range(6)]
    flow = []
    for face in range(6):
        mode = modes[face // 2 + 1]
        own = modes[0] - mode if face % 2 == 0 else modes[0] + mode
        rows = pl.ds(face * groups, groups)
        flow.append(flux[face] * jnp.where(flags[rows, :] == 1, own, across[rows, :]))
    step = ratio[...]
    out[pl.ds(0, groups, stride=4), :] = modes[0] - step * (
        flow[0] + flow[1] + flow[2] + flow[3] + flow[4] + flow[5]
    )
    for mode in range(1, 4):
        lo, hi = 2 * mode - 2, 2 * mode - 1
        volume = 0.5 * (flux[hi] - flux[lo]) * modes[0]
        out[pl.ds(mode, groups, stride=4), :] = modes[mode] + 3.0 * step * (
            volume - (flow[hi] - flow[lo])
        )


whole = pl.BlockSpec(memory_space=pltpu.VMEM)
far = pl.BlockSpec(memory_space=pl.ANY)


def call(kernel, outs, specs, scratch=(), flops=0, traffic=0, out_specs=None, aliases=None):
    return pl.pallas_call(
        kernel,
        out_shape=outs,
        in_specs=specs,
        out_specs=[whole] * len(outs) if out_specs is None else out_specs,
        scratch_shapes=list(scratch),
        input_output_aliases=aliases or {},
        compiler_params=pltpu.CompilerParams(vmem_limit_bytes=vmem_bytes),
        cost_estimate=pl.CostEstimate(flops=flops, bytes_accessed=traffic, transcendentals=0),
    )


def keep_far(array):
    return pltpu.with_memory_space_constraint(array, pltpu.HBM)


def by_cells(array):
    return array.reshape(-1, lane_width)


def by_groups(array):
    rows = array.shape[0]
    return jnp.swapaxes(array.reshape(rows, -1, lane_width), 0, 1).reshape(-1, lane_width)


def per_device(
    mesh_dims,
    plans,
    trace_guess,
    trace_rhs,
    block_inverse,
    coupling,
    block_neighbours,
    block_send,
    cell_faces,
    face_coeff,
    cell_source,
    cell_neighbours,
    upwind_flags,
    cell_send,
    saturation,
    step_ratio,
):
    guess = trace_guess[0, 0]
    rhs = trace_rhs[0, 0]
    inverse = block_inverse[0, 0]
    couple = coupling[0, 0]
    links = block_neighbours[0, 0].T
    sends = block_send[0, 0].T
    blocks, columns, size = guess.shape
    blocks_sent = sends.shape[0]
    halo_rows = blocks_sent * columns
    extended_blocks = blocks + 4 * blocks_sent
    sat = by_groups(saturation[0, 0])
    cell_list = by_groups(cell_send[0, 0])
    halves = cell_list.shape[0] // 4
    groups = sat.shape[0] // 4
    half, single = jnp.bfloat16, jnp.float32

    def like(array):
        return jax.ShapeDtypeStruct(array.shape, array.dtype)

    widened = (extended_blocks, columns, size)
    *packed, extended = call(
        functools.partial(pack_kernel, mesh_dims),
        [jax.ShapeDtypeStruct((halo_rows + tail_rows, size), half)] * 4
        + [jax.ShapeDtypeStruct(widened, half)],
        [far] * 4,
        [
            pltpu.VMEM(sends.shape, jnp.int32),
            pltpu.VMEM(guess.shape, single),
            pltpu.VMEM(cell_list.shape, jnp.int32),
            pltpu.VMEM(sat.shape, single),
            pltpu.VMEM((4 * halves, lane_width), single),
            pltpu.SemaphoreType.DMA((3 + blocks,)),
        ],
    )(*map(keep_far, (sends, guess, cell_list, sat)))
    arrived = trade(packed, plans)

    remote = [
        couple,
        inverse,
        rhs,
        by_cells(cell_faces[0, 0]),
        by_cells(face_coeff[0, 0]),
        by_cells(cell_source[0]),
        by_cells(cell_neighbours[0, 0]),
        by_cells(upwind_flags[0, 0]),
        sat,
        by_cells(step_ratio[0]),
        links,
        sends,
    ]
    (
        couple,
        inverse,
        rhs,
        cell_faces,
        coeff,
        source,
        neighbours,
        flags,
        sat,
        ratio,
        links,
        sends,
        near0,
        near1,
    ) = call(
        functools.partial(fetch_kernel, len(remote)),
        [like(array) for array in remote] + [like(sends)] * 2,
        [far] * (1 + len(remote)),
        [pltpu.SemaphoreType.DMA((len(remote),))],
        traffic=4 * guess.size,
    )(packed[0], *map(keep_far, remote))

    sweep_flops = 6 * blocks * columns * size * size
    extended, *packed = call(
        functools.partial(first_edge_kernel, mesh_dims),
        [like(extended)] + [jax.ShapeDtypeStruct((halo_rows, size), half)] * 4,
        [whole] * 11,
        flops=sweep_flops // 2,
        aliases={3: 0},
    )(sends, near0, near1, extended, *arrived, couple, inverse, rhs)
    swept = trade(packed, plans)

    tails = [piece[halo_rows:] for piece in arrived]
    cell_rows = -(-(groups + halves) // 8) * 8
    extended, across = call(
        functools.partial(first_sweep_kernel, mesh_dims, halves),
        [like(extended), jax.ShapeDtypeStruct(neighbours.shape, single)],
        [whole] * 11,
        [pltpu.VMEM((6 * cell_rows, lane_width), single)],
        sweep_flops,
    )(links, extended, couple, inverse, rhs, sat, neighbours, *tails)

    extended, *packed = call(
        functools.partial(second_edge_kernel, mesh_dims),
        [like(extended)] + [jax.ShapeDtypeStruct((tail_rows, size), half)] * 4,
        [whole] * 11,
        flops=sweep_flops // 16,
        aliases={3: 0},
    )(sends, near0, near1, extended, *swept, couple, inverse, rhs)
    edges = trade(packed, plans)

    traces, partial = call(
        second_sweep_kernel,
        [jax.ShapeDtypeStruct(guess.shape, single), jax.ShapeDtypeStruct(coeff.shape, single)],
        [whole] * 6,
        [
            pltpu.VMEM(guess.shape, single),
            pltpu.VMEM((blocks, size), single),
            pltpu.SemaphoreType.DMA((blocks,)),
        ],
        sweep_flops,
        out_specs=[far, whole],
    )(links, extended, couple, inverse, rhs, cell_faces)

    (following,) = call(
        functools.partial(cells_kernel, mesh_dims, blocks, blocks_sent),
        [like(sat)],
        [whole] * 12,
        [pltpu.VMEM((4 * blocks_sent, lane_width), single)],
    )(partial, *edges[2:], *edges[:2], across, cell_faces, coeff, source, flags, sat, ratio)
    saturation_next = jnp.swapaxes(following.reshape(groups, 4, lane_width), 0, 1).reshape(4, -1)
    return traces[None, None], saturation_next[None, None]


def solution(mesh):
    mesh_dims = (mesh.shape["wide"], mesh.shape["narrow"])

    def spec(rank):
        return P("wide", "narrow", *([None] * (rank - 2)))

    placed = tuple(spec(rank) for rank in (5, 5, 5, 6, 4, 4, 4, 4, 3, 4, 4, 4, 4, 3))
    return jax.shard_map(
        functools.partial(per_device, mesh_dims, pairings(*mesh_dims)),
        mesh=mesh,
        in_specs=placed,
        out_specs=(spec(5), spec(4)),
        check_vma=False,
    )
```

```python
import functools

import jax
import jax.numpy as jnp
from jax import lax
from jax.experimental import pallas as pl
from jax.experimental.pallas import tpu as pltpu
from jax.sharding import PartitionSpec as P

lane_width = 128
tail_rows = 16
vmem_bytes = 24 * 1024 * 1024
axes = ("wide", "narrow")


def pairings(wide, narrow):
    def number(i, j):
        return i * narrow + j

    def close(pairs, partner_of):
        taken = {d for pair in pairs for d in pair}
        for i in range(wide):
            for j in range(narrow):
                partner = partner_of(i, j)
                if number(i, j) in taken:
                    continue
                if 0 <= partner[0] < wide and 0 <= partner[1] < narrow:
                    if number(*partner) not in taken:
                        pairs.append((number(i, j), number(*partner)))
                        taken |= {number(i, j), number(*partner)}
        moves = [(a, b) for a, b in pairs] + [(b, a) for a, b in pairs if a != b]
        sources = {a for a, _ in moves}
        return moves + [(d, d) for d in range(wide * narrow) if d not in sources]

    plans = []
    for first in (0, 1):
        pairs = [
            (number(i, j), number(i + 1, j))
            for i in range(first, wide - 1, 2)
            for j in range(narrow)
        ]
        plans.append(close(pairs, lambda i, j: (i, j ^ 1)))
    for first in (0, 1):
        pairs = [
            (number(i, j), number(i, j + 1))
            for i in range(wide)
            for j in range(first, narrow - 1, 2)
        ]
        plans.append(close(pairs, lambda i, j: (i, narrow - 1 - j)))
    return plans


def trade(pieces, plans):
    return [lax.ppermute(piece, axes, plan) for piece, plan in zip(pieces, plans)]


def sides_of(wide, narrow):
    found = []
    for base, axis, count in ((0, "wide", wide), (2, "narrow", narrow)):
        here = lax.axis_index(axis)
        for first in (0, 1):
            partner = ((here + first) ^ 1) - first
            side = base + jnp.where(partner > here, 1, 0)
            found.append((side, (partner >= 0) & (partner < count)))
    return found


def spread(row):
    return jnp.broadcast_to(row, (8, lane_width))


def take_lanes(row, low):
    return jnp.take_along_axis(row, low, axis=1, mode="promise_in_bounds")


def pack_kernel(
    mesh_dims, sends_far, guess_far, list_far, sat_far,
    out0, out1, out2, out3, guess,
    sends, cell_list, sat, picked, arrivals,
):
    places = sides_of(*mesh_dims)
    blocks, size = guess.shape[0], guess.shape[1]
    copies = [
        pltpu.make_async_copy(far, near, arrivals.at[slot])
        for slot, (far, near) in enumerate(
            ((list_far, cell_list), (sat_far, sat), (sends_far, sends))
        )
    ]
    loads = [
        pltpu.make_async_copy(guess_far.at[block], guess.at[block], arrivals.at[3 + block])
        for block in range(blocks)
    ]
    for copy in copies + loads:
        copy.start()
    for copy in copies:
        copy.wait()
    blocks_sent = sends.shape[0]
    groups = sat.shape[0] // 4
    lists = cell_list.shape[0]
    halves = lists // 4
    index = cell_list[...]
    high = index >> 7
    low = index & (lane_width - 1)
    found = jnp.zeros(index.shape, jnp.float32)
    for group in range(groups):
        modes = sat[pl.ds(group * 4, 4), :]
        mean, along_x, along_y = modes[0:1], modes[1:2], modes[2:3]
        four = jnp.concatenate([mean - along_x, mean + along_x, mean - along_y, mean + along_y], 0)
        rows = jnp.concatenate([four] * halves, 0)
        found = jnp.where(high == group, take_lanes(rows, low), found)
    picked[...] = found
    for (side, _), out in zip(places, (out0, out1, out2, out3)):
        values = [picked[pl.ds(half * 4 + side, 1), :] for half in range(halves)]
        coarse = [value.astype(jnp.bfloat16).astype(jnp.float32) for value in values]
        fine = [value - rounded for value, rounded in zip(values, coarse)]
        blank = jnp.zeros((tail_rows - 2 * halves, lane_width), jnp.float32)
        out[pl.ds(blocks_sent * size, tail_rows), :] = jnp.concatenate(
            coarse + fine + [blank], 0
        ).astype(jnp.bfloat16)
    listed = listed_blocks(sends, places)
    for load in loads:
        load.wait()
    for picks, out in zip(listed, (out0, out1, out2, out3)):
        for slot, block in enumerate(picks):
            out[pl.ds(slot * size, size), :] = guess[block].astype(jnp.bfloat16)


def listed_blocks(sends, places):
    value = sends[...]
    count = value.shape[0]
    sides = [[value[slot, side] for slot in range(count)] for side in range(4)]
    found = []
    for pairing, (side, _) in enumerate(places):
        first = 0 if pairing < 2 else 2
        found.append(
            [jnp.where(side == first, a, b) for a, b in zip(sides[first], sides[first + 1])]
        )
    return found


def flatten(listed, links):
    near0, near1 = links
    blocks = [block for picks in listed for block in picks]
    pairs = [pair for picks in zip(near0, near1) for pair in zip(*picks)]
    return blocks, pairs


def linked_blocks(links):
    value = links[...]
    return [[value[k, block] for k in range(2)] for block in range(value.shape[1])]


def in_parts(links):
    pairs = linked_blocks(links)
    for start in range(0, len(pairs), 8):
        yield range(start, min(start + 8, len(pairs))), pairs[start : start + 8]


def fetch_kernel(count, *refs):
    guess, fars, nears = refs[0], refs[1 : 1 + count], refs[1 + count : 1 + 2 * count]
    near0, near1, extended, arrivals = refs[1 + 2 * count :]
    copies = [
        pltpu.make_async_copy(far, near, arrivals.at[slot])
        for slot, (far, near) in enumerate(zip(fars, nears))
    ]
    for copy in copies:
        copy.start()
    for block in range(guess.shape[0]):
        extended[block] = guess[block].astype(jnp.bfloat16)
    for copy in copies:
        copy.wait()
    links, sends = nears[-2][...], nears[-1][...]
    for k, near in enumerate((near0, near1)):
        chosen = jnp.zeros_like(sends)
        for block in range(links.shape[1]):
            chosen = jnp.where(sends == block, links[k, block], chosen)
        near[...] = chosen


def product(left, right):
    return lax.dot_general(
        left, right, (((1,), (1,)), ((), ())), preferred_element_type=jnp.float32
    )


def relax(extended, couple, inverse, rhs, blocks, links, rows):
    resid = []
    for block, pair in zip(blocks, links):
        near = jnp.concatenate([extended[link, 0:rows, :] for link in pair], 1)
        matrix = jnp.concatenate([couple[block, k] for k in range(len(pair))], 1)
        resid.append((rhs[block, 0:rows, :] - product(near, matrix)).astype(jnp.bfloat16))
    return [product(part, inverse[block]) for part, block in zip(resid, blocks)]


def land(extended, places, arrived, blocks_sent):
    own_count = extended.shape[0] - 4 * blocks_sent
    size = extended.shape[1]
    for (side, exists), came in zip(places, arrived):
        for block in range(blocks_sent):
            value = came[pl.ds(block * size, size), :]
            value = jnp.where(exists, value, jnp.zeros_like(value))
            extended[own_count + side * blocks_sent + block] = value


def first_edge_kernel(
    mesh_dims, sends, near0, near1, _, in0, in1, in2, in3, couple, inverse, rhs,
    extended, out0, out1, out2, out3,
):
    places = sides_of(*mesh_dims)
    size = extended.shape[1]
    listed = listed_blocks(sends, places)
    links = [listed_blocks(near, places) for near in (near0, near1)]
    land(extended, places, (in0, in1, in2, in3), sends.shape[0])
    fresh = relax(extended, couple, inverse, rhs, *flatten(listed, links), size)
    slots = sends.shape[0]
    for pairing, out in enumerate((out0, out1, out2, out3)):
        for slot in range(slots):
            value = fresh[pairing * slots + slot]
            out[pl.ds(slot * size, size), :] = value.astype(jnp.bfloat16)


def look_up(table, first_row, rows, high, low, value):
    for row in rows:
        got = take_lanes(spread(table[pl.ds(first_row + row, 1), :]), low)
        value = jnp.where(high == row, got, value)
    return value


def nothing():
    return jnp.zeros((8, lane_width), jnp.float32)


def first_sweep_kernel(
    mesh_dims, halves, links, extended, couple, inverse, rhs,
    sat, neighbours, tail0, tail1, tail2, tail3,
    smoothed, across, across_rows,
):
    places = sides_of(*mesh_dims)
    groups = sat.shape[0] // 4
    stride = across_rows.shape[0] // 6
    modes = [sat[pl.ds(mode, groups, stride=4), :] for mode in range(4)]
    for (side, exists), came in zip(places, (tail0, tail1, tail2, tail3)):
        value = came[...].astype(jnp.float32)
        value = value[0:halves] + value[halves : 2 * halves]
        value = jnp.where(exists, value, jnp.zeros_like(value))
        for half in range(halves):
            across_rows[pl.ds(side * stride + groups + half, 1), :] = value[half : half + 1]
    for face in range(6):
        mode = modes[face // 2 + 1]
        across_rows[pl.ds(face * stride, groups), :] = (
            modes[0] + mode if face % 2 == 0 else modes[0] - mode
        )
    for blocks, pairs in in_parts(links):
        fresh = relax(extended, couple, inverse, rhs, blocks, pairs, extended.shape[1])
        for block, value in zip(blocks, fresh):
            smoothed[block] = value.astype(jnp.bfloat16)
    for face in range(6):
        for start in range(0, groups, 8):
            index = neighbours[pl.ds(face * groups + start, 8), :]
            high, low = index >> 7, index & (lane_width - 1)
            if 0 < face < 4:
                high = jnp.where(high >= groups, high - face * halves, high)
            rows = range(groups + halves if face < 4 else groups)
            across[pl.ds(face * groups + start, 8), :] = look_up(
                across_rows, face * stride, rows, high, low, nothing()
            )


def second_edge_kernel(
    mesh_dims, sends, near0, near1, _, in1, in0, in3, in2, couple, inverse, rhs,
    extended, out0, out1, out2, out3,
):
    places = sides_of(*mesh_dims)
    listed = listed_blocks(sends, places)
    links = [listed_blocks(near, places) for near in (near0, near1)]
    land(extended, places, (in0, in1, in2, in3), sends.shape[0])
    fresh = relax(extended, couple, inverse, rhs, *flatten(listed, links), tail_rows)
    slots = sends.shape[0]
    for pairing, out in enumerate((out0, out1, out2, out3)):
        rows = [fresh[pairing * slots + slot][0:1, :] for slot in range(slots)]
        blank = jnp.zeros((tail_rows - len(rows), lane_width), jnp.float32)
        out[...] = jnp.concatenate(rows + [blank], 0).astype(jnp.bfloat16)


def second_sweep_kernel(
    links, extended, couple, inverse, rhs, cell_faces,
    traces, partial, fresh, column, departures,
):
    stores = []
    for blocks, pairs in in_parts(links):
        values = relax(extended, couple, inverse, rhs, blocks, pairs, extended.shape[1])
        for block, value in zip(blocks, values):
            fresh[block] = value
            stores.append(
                pltpu.make_async_copy(fresh.at[block], traces.at[block], departures.at[block])
            )
            stores[block].start()
            column[pl.ds(block, 1), :] = value[0:1].astype(jnp.bfloat16).astype(jnp.float32)
    for start in range(0, cell_faces.shape[0], 8):
        index = cell_faces[pl.ds(start, 8), :]
        rows = range(column.shape[0])
        partial[pl.ds(start, 8), :] = look_up(
            column, 0, rows, index >> 7, index & (lane_width - 1), nothing()
        )
    for store in stores:
        store.wait()


def cells_kernel(
    mesh_dims, blocks, blocks_sent, partial, in1, in3, in0, in2, across,
    cell_faces, coeff, source, flags, sat, ratio, out, faces,
):
    places = sides_of(*mesh_dims)
    groups = sat.shape[0] // 4
    for (side, exists), came in zip(places, (in0, in1, in2, in3)):
        value = came[...].astype(jnp.float32)[0:blocks_sent]
        value = jnp.where(exists, value, jnp.zeros_like(value))
        for block in range(blocks_sent):
            faces[pl.ds(side * blocks_sent + block, 1), :] = value[block : block + 1]
    modes = [sat[pl.ds(mode, groups, stride=4), :] for mode in range(4)]
    weights = [coeff[pl.ds(face * groups, groups), :] for face in range(6)]
    traces = []
    for face in range(6):
        parts = []
        for start in range(0, groups, 8):
            rows = pl.ds(face * groups + start, 8)
            index = cell_faces[rows, :]
            high, low = (index >> 7) - blocks, index & (lane_width - 1)
            parts.append(look_up(faces, 0, range(4 * blocks_sent), high, low, partial[rows, :]))
        traces.append(jnp.concatenate(parts, 0))
    total = weights[0]
    gained = source[...] + weights[0] * traces[0]
    for face in range(1, 6):
        total = total + weights[face]
        gained = gained + weights[face] * traces[face]
    pressure = gained / total
    flux = [weights[face] * (pressure - traces[face]) for face in range(6)]
    flow = []
    for face in range(6):
        mode = modes[face // 2 + 1]
        own = modes[0] - mode if face % 2 == 0 else modes[0] + mode
        rows = pl.ds(face * groups, groups)
        flow.append(flux[face] * jnp.where(flags[rows, :] == 1, own, across[rows, :]))
    step = ratio[...]
    out[pl.ds(0, groups, stride=4), :] = modes[0] - step * (
        flow[0] + flow[1] + flow[2] + flow[3] + flow[4] + flow[5]
    )
    for mode in range(1, 4):
        lo, hi = 2 * mode - 2, 2 * mode - 1
        volume = 0.5 * (flux[hi] - flux[lo]) * modes[0]
        out[pl.ds(mode, groups, stride=4), :] = modes[mode] + 3.0 * step * (
            volume - (flow[hi] - flow[lo])
        )


whole = pl.BlockSpec(memory_space=pltpu.VMEM)
far = pl.BlockSpec(memory_space=pl.ANY)


def call(kernel, outs, specs, scratch=(), flops=0, traffic=0, out_specs=None, aliases=None):
    return pl.pallas_call(
        kernel,
        out_shape=outs,
        in_specs=specs,
        out_specs=[whole] * len(outs) if out_specs is None else out_specs,
        scratch_shapes=list(scratch),
        input_output_aliases=aliases or {},
        compiler_params=pltpu.CompilerParams(vmem_limit_bytes=vmem_bytes),
        cost_estimate=pl.CostEstimate(flops=flops, bytes_accessed=traffic, transcendentals=0),
    )


def keep_far(array):
    return pltpu.with_memory_space_constraint(array, pltpu.HBM)


def by_cells(array):
    return array.reshape(-1, lane_width)


def by_groups(array):
    rows = array.shape[0]
    return jnp.swapaxes(array.reshape(rows, -1, lane_width), 0, 1).reshape(-1, lane_width)


def per_device(
    mesh_dims,
    plans,
    trace_guess,
    trace_rhs,
    block_inverse,
    coupling,
    block_neighbours,
    block_send,
    cell_faces,
    face_coeff,
    cell_source,
    cell_neighbours,
    upwind_flags,
    cell_send,
    saturation,
    step_ratio,
):
    guess = trace_guess[0, 0]
    rhs = trace_rhs[0, 0]
    inverse = block_inverse[0, 0]
    couple = coupling[0, 0]
    links = block_neighbours[0, 0].T
    sends = block_send[0, 0].T
    blocks, columns, size = guess.shape
    blocks_sent = sends.shape[0]
    halo_rows = blocks_sent * columns
    extended_blocks = blocks + 4 * blocks_sent
    sat = by_groups(saturation[0, 0])
    cell_list = by_groups(cell_send[0, 0])
    halves = cell_list.shape[0] // 4
    groups = sat.shape[0] // 4
    half, single = jnp.bfloat16, jnp.float32

    def like(array):
        return jax.ShapeDtypeStruct(array.shape, array.dtype)

    widened = (extended_blocks, columns, size)
    *packed, guess = call(
        functools.partial(pack_kernel, mesh_dims),
        [jax.ShapeDtypeStruct((halo_rows + tail_rows, size), half)] * 4 + [like(guess)],
        [far] * 4,
        [
            pltpu.VMEM(sends.shape, jnp.int32),
            pltpu.VMEM(cell_list.shape, jnp.int32),
            pltpu.VMEM(sat.shape, single),
            pltpu.VMEM((4 * halves, lane_width), single),
            pltpu.SemaphoreType.DMA((3 + blocks,)),
        ],
    )(*map(keep_far, (sends, guess, cell_list, sat)))
    arrived = trade(packed, plans)

    remote = [
        couple,
        inverse,
        rhs,
        by_cells(cell_faces[0, 0]),
        by_cells(face_coeff[0, 0]),
        by_cells(cell_source[0]),
        by_cells(cell_neighbours[0, 0]),
        by_cells(upwind_flags[0, 0]),
        sat,
        by_cells(step_ratio[0]),
        links,
        sends,
    ]
    (
        couple,
        inverse,
        rhs,
        cell_faces,
        coeff,
        source,
        neighbours,
        flags,
        sat,
        ratio,
        links,
        sends,
        near0,
        near1,
        extended,
    ) = call(
        functools.partial(fetch_kernel, len(remote)),
        [like(array) for array in remote]
        + [like(sends)] * 2
        + [jax.ShapeDtypeStruct(widened, half)],
        [whole] + [far] * len(remote),
        [pltpu.SemaphoreType.DMA((len(remote),))],
        traffic=4 * guess.size,
    )(guess, *map(keep_far, remote))

    sweep_flops = 6 * blocks * columns * size * size
    extended, *packed = call(
        functools.partial(first_edge_kernel, mesh_dims),
        [like(extended)] + [jax.ShapeDtypeStruct((halo_rows, size), half)] * 4,
        [whole] * 11,
        flops=sweep_flops // 2,
        aliases={3: 0},
    )(sends, near0, near1, extended, *arrived, couple, inverse, rhs)
    swept = trade(packed, plans)

    tails = [piece[halo_rows:] for piece in arrived]
    cell_rows = -(-(groups + halves) // 8) * 8
    extended, across = call(
        functools.partial(first_sweep_kernel, mesh_dims, halves),
        [like(extended), jax.ShapeDtypeStruct(neighbours.shape, single)],
        [whole] * 11,
        [pltpu.VMEM((6 * cell_rows, lane_width), single)],
        sweep_flops,
    )(links, extended, couple, inverse, rhs, sat, neighbours, *tails)

    extended, *packed = call(
        functools.partial(second_edge_kernel, mesh_dims),
        [like(extended)] + [jax.ShapeDtypeStruct((tail_rows, size), half)] * 4,
        [whole] * 11,
        flops=sweep_flops // 16,
        aliases={3: 0},
    )(sends, near0, near1, extended, *(swept[k] for k in (1, 0, 3, 2)), couple, inverse, rhs)
    edges = trade(packed, plans)

    traces, partial = call(
        second_sweep_kernel,
        [jax.ShapeDtypeStruct(guess.shape, single), jax.ShapeDtypeStruct(coeff.shape, single)],
        [whole] * 6,
        [
            pltpu.VMEM(guess.shape, single),
            pltpu.VMEM((blocks, size), single),
            pltpu.SemaphoreType.DMA((blocks,)),
        ],
        sweep_flops,
        out_specs=[far, whole],
    )(links, extended, couple, inverse, rhs, cell_faces)

    (following,) = call(
        functools.partial(cells_kernel, mesh_dims, blocks, blocks_sent),
        [like(sat)],
        [whole] * 12,
        [pltpu.VMEM((4 * blocks_sent, lane_width), single)],
    )(partial, *(edges[k] for k in (1, 3, 0, 2)), across, cell_faces, coeff, source, flags, sat, ratio)
    saturation_next = jnp.swapaxes(following.reshape(groups, 4, lane_width), 0, 1).reshape(4, -1)
    return traces[None, None], saturation_next[None, None]


def solution(mesh):
    mesh_dims = (mesh.shape["wide"], mesh.shape["narrow"])

    def spec(rank):
        return P("wide", "narrow", *([None] * (rank - 2)))

    placed = tuple(spec(rank) for rank in (5, 5, 5, 6, 4, 4, 4, 4, 3, 4, 4, 4, 4, 3))
    return jax.shard_map(
        functools.partial(per_device, mesh_dims, pairings(*mesh_dims)),
        mesh=mesh,
        in_specs=placed,
        out_specs=(spec(5), spec(4)),
        check_vma=False,
    )
```

```python
import functools

import jax
import jax.numpy as jnp
from jax import lax
from jax.experimental import pallas as pl
from jax.experimental.pallas import tpu as pltpu
from jax.sharding import PartitionSpec as P

lane_width = 128
tail_rows = 16
vmem_bytes = 24 * 1024 * 1024
axes = ("wide", "narrow")


def pairings(wide, narrow):
    def number(i, j):
        return i * narrow + j

    def close(pairs, partner_of):
        taken = {d for pair in pairs for d in pair}
        for i in range(wide):
            for j in range(narrow):
                partner = partner_of(i, j)
                if number(i, j) in taken:
                    continue
                if 0 <= partner[0] < wide and 0 <= partner[1] < narrow:
                    if number(*partner) not in taken:
                        pairs.append((number(i, j), number(*partner)))
                        taken |= {number(i, j), number(*partner)}
        moves = [(a, b) for a, b in pairs] + [(b, a) for a, b in pairs if a != b]
        sources = {a for a, _ in moves}
        return moves + [(d, d) for d in range(wide * narrow) if d not in sources]

    plans = []
    for first in (0, 1):
        pairs = [
            (number(i, j), number(i + 1, j))
            for i in range(first, wide - 1, 2)
            for j in range(narrow)
        ]
        plans.append(close(pairs, lambda i, j: (i, j ^ 1)))
    for first in (0, 1):
        pairs = [
            (number(i, j), number(i, j + 1))
            for i in range(wide)
            for j in range(first, narrow - 1, 2)
        ]
        plans.append(close(pairs, lambda i, j: (i, narrow - 1 - j)))
    return plans


def trade(pieces, plans):
    return [lax.ppermute(piece, axes, plan) for piece, plan in zip(pieces, plans)]


def sides_of(wide, narrow):
    found = []
    for base, axis, count in ((0, "wide", wide), (2, "narrow", narrow)):
        here = lax.axis_index(axis)
        for first in (0, 1):
            partner = ((here + first) ^ 1) - first
            side = base + jnp.where(partner > here, 1, 0)
            found.append((side, (partner >= 0) & (partner < count)))
    return found


def spread(row):
    return jnp.broadcast_to(row, (8, lane_width))


def take_lanes(row, low):
    return jnp.take_along_axis(row, low, axis=1, mode="promise_in_bounds")


def pack_kernel(
    mesh_dims, sends_far, guess_far, list_far, sat_far,
    out0, out1, out2, out3, guess,
    sends, cell_list, sat, picked, arrivals,
):
    places = sides_of(*mesh_dims)
    blocks, size = guess.shape[0], guess.shape[1]
    copies = [
        pltpu.make_async_copy(far, near, arrivals.at[slot])
        for slot, (far, near) in enumerate(
            ((list_far, cell_list), (sat_far, sat), (sends_far, sends))
        )
    ]
    loads = [
        pltpu.make_async_copy(guess_far.at[block], guess.at[block], arrivals.at[3 + block])
        for block in range(blocks)
    ]
    for copy in copies + loads:
        copy.start()
    for copy in copies:
        copy.wait()
    blocks_sent = sends.shape[0]
    groups = sat.shape[0] // 4
    lists = cell_list.shape[0]
    halves = lists // 4
    index = cell_list[...]
    high = index >> 7
    low = index & (lane_width - 1)
    found = jnp.zeros(index.shape, jnp.float32)
    for group in range(groups):
        modes = sat[pl.ds(group * 4, 4), :]
        mean, along_x, along_y = modes[0:1], modes[1:2], modes[2:3]
        four = jnp.concatenate([mean - along_x, mean + along_x, mean - along_y, mean + along_y], 0)
        rows = jnp.concatenate([four] * halves, 0)
        found = jnp.where(high == group, take_lanes(rows, low), found)
    picked[...] = found
    for (side, _), out in zip(places, (out0, out1, out2, out3)):
        values = [picked[pl.ds(half * 4 + side, 1), :] for half in range(halves)]
        coarse = [value.astype(jnp.bfloat16).astype(jnp.float32) for value in values]
        fine = [value - rounded for value, rounded in zip(values, coarse)]
        blank = jnp.zeros((tail_rows - 2 * halves, lane_width), jnp.float32)
        out[pl.ds(blocks_sent * size, tail_rows), :] = jnp.concatenate(
            coarse + fine + [blank], 0
        ).astype(jnp.bfloat16)
    listed = listed_blocks(sends, places)
    for load in loads:
        load.wait()
    for picks, out in zip(listed, (out0, out1, out2, out3)):
        for slot, block in enumerate(picks):
            out[pl.ds(slot * size, size), :] = guess[block].astype(jnp.bfloat16)


def listed_blocks(sends, places):
    value = sends[...]
    count = value.shape[0]
    sides = [[value[slot, side] for slot in range(count)] for side in range(4)]
    found = []
    for pairing, (side, _) in enumerate(places):
        first = 0 if pairing < 2 else 2
        found.append(
            [jnp.where(side == first, a, b) for a, b in zip(sides[first], sides[first + 1])]
        )
    return found


def listed_links(near0, near1):
    values = near0[...], near1[...]
    slots, pairings = values[0].shape
    return [
        [value[slot, pairing] for value in values]
        for pairing in range(pairings)
        for slot in range(slots)
    ]


def linked_blocks(links):
    value = links[...]
    return [[value[k, block] for k in range(2)] for block in range(value.shape[1])]


def in_parts(links):
    pairs = linked_blocks(links)
    for start in range(0, len(pairs), 8):
        yield range(start, min(start + 8, len(pairs))), pairs[start : start + 8]


def fetch_kernel(mesh_dims, count, *refs):
    guess, fars, nears = refs[0], refs[1 : 1 + count], refs[1 + count : 1 + 2 * count]
    near0, near1, extended, couple_listed, inverse_listed, rhs_listed, arrivals = refs[
        1 + 2 * count :
    ]
    copies = [
        pltpu.make_async_copy(far, near, arrivals.at[slot])
        for slot, (far, near) in enumerate(zip(fars, nears))
    ]
    for copy in copies:
        copy.start()
    for block in range(guess.shape[0]):
        extended[block] = guess[block].astype(jnp.bfloat16)
    for copy in copies:
        copy.wait()
    links, sends = nears[-2][...], nears[-1][...]
    columns = []
    for pairing, (side, _) in enumerate(sides_of(*mesh_dims)):
        first = 0 if pairing < 2 else 2
        columns.append(
            jnp.where(side == first, sends[:, first : first + 1], sends[:, first + 1 : first + 2])
        )
    listed = jnp.concatenate(columns, 1)
    for k, near in enumerate((near0, near1)):
        chosen = jnp.zeros_like(listed)
        for block in range(links.shape[1]):
            chosen = jnp.where(listed == block, links[k, block], chosen)
        near[...] = chosen
    couple, inverse, rhs = nears[:3]
    slots = listed.shape[0]
    for place in range(couple_listed.shape[0]):
        block = listed[place % slots, place // slots]
        couple_listed[place] = couple[block]
        inverse_listed[place] = inverse[block]
        rhs_listed[place] = rhs[block]


def product(left, right):
    return lax.dot_general(
        left, right, (((1,), (1,)), ((), ())), preferred_element_type=jnp.float32
    )


def relax(extended, couple, inverse, rhs, blocks, links, rows):
    resid = []
    for block, pair in zip(blocks, links):
        near = jnp.concatenate([extended[link, 0:rows, :] for link in pair], 1)
        matrix = jnp.concatenate([couple[block, k] for k in range(len(pair))], 1)
        resid.append((rhs[block, 0:rows, :] - product(near, matrix)).astype(jnp.bfloat16))
    return [product(part, inverse[block]) for part, block in zip(resid, blocks)]


def land(extended, places, arrived, blocks_sent, rows):
    own_count = extended.shape[0] - 4 * blocks_sent
    size = extended.shape[1]
    for (side, exists), came in zip(places, arrived):
        for block in range(blocks_sent):
            value = came[pl.ds(block * size, rows), :]
            value = jnp.where(exists, value, jnp.zeros_like(value))
            extended[own_count + side * blocks_sent + block, 0:rows, :] = value


def first_edge_kernel(
    mesh_dims, near0, near1, _, in1, in0, in2, in3, couple, inverse, rhs,
    extended, out0, out1, out2, out3,
):
    size = extended.shape[1]
    slots = near0.shape[0]
    links = listed_links(near0, near1)
    land(extended, sides_of(*mesh_dims), (in0, in1, in2, in3), slots, size)
    fresh = relax(extended, couple, inverse, rhs, range(len(links)), links, size)
    for pairing, out in enumerate((out0, out1, out2, out3)):
        for slot in range(slots):
            value = fresh[pairing * slots + slot]
            out[pl.ds(slot * size, size), :] = value.astype(jnp.bfloat16)


def look_up(table, first_row, rows, high, low, value):
    for row in rows:
        got = take_lanes(spread(table[pl.ds(first_row + row, 1), :]), low)
        value = jnp.where(high == row, got, value)
    return value


def nothing():
    return jnp.zeros((8, lane_width), jnp.float32)


def first_sweep_kernel(
    mesh_dims, halves, links, extended, couple, inverse, rhs,
    sat, neighbours, tail0, tail1, tail2, tail3,
    smoothed, across, across_rows,
):
    places = sides_of(*mesh_dims)
    groups = sat.shape[0] // 4
    stride = across_rows.shape[0] // 6
    modes = [sat[pl.ds(mode, groups, stride=4), :] for mode in range(4)]
    for (side, exists), came in zip(places, (tail0, tail1, tail2, tail3)):
        value = came[...].astype(jnp.float32)
        value = value[0:halves] + value[halves : 2 * halves]
        value = jnp.where(exists, value, jnp.zeros_like(value))
        for half in range(halves):
            across_rows[pl.ds(side * stride + groups + half, 1), :] = value[half : half + 1]
    for face in range(6):
        mode = modes[face // 2 + 1]
        across_rows[pl.ds(face * stride, groups), :] = (
            modes[0] + mode if face % 2 == 0 else modes[0] - mode
        )
    for blocks, pairs in in_parts(links):
        fresh = relax(extended, couple, inverse, rhs, blocks, pairs, extended.shape[1])
        for block, value in zip(blocks, fresh):
            smoothed[block] = value.astype(jnp.bfloat16)
    for face in range(6):
        for start in range(0, groups, 8):
            index = neighbours[pl.ds(face * groups + start, 8), :]
            high, low = index >> 7, index & (lane_width - 1)
            if 0 < face < 4:
                high = jnp.where(high >= groups, high - face * halves, high)
            rows = range(groups + halves if face < 4 else groups)
            across[pl.ds(face * groups + start, 8), :] = look_up(
                across_rows, face * stride, rows, high, low, nothing()
            )


def second_edge_kernel(
    mesh_dims, near0, near1, _, in1, in0, in2, in3, couple, inverse, rhs,
    extended, out0, out1, out2, out3,
):
    slots = near0.shape[0]
    links = listed_links(near0, near1)
    land(extended, sides_of(*mesh_dims), (in0, in1, in2, in3), slots, tail_rows)
    fresh = relax(extended, couple, inverse, rhs, range(len(links)), links, tail_rows)
    for pairing, out in enumerate((out0, out1, out2, out3)):
        rows = [fresh[pairing * slots + slot][0:1, :] for slot in range(slots)]
        blank = jnp.zeros((tail_rows - len(rows), lane_width), jnp.float32)
        out[...] = jnp.concatenate(rows + [blank], 0).astype(jnp.bfloat16)


def second_sweep_kernel(
    mesh_dims, blocks_sent, links, _, in0, in1, in2, in3, couple, inverse, rhs, cell_faces,
    traces, partial, extended, fresh, column, departures,
):
    land(extended, sides_of(*mesh_dims), (in0, in1, in2, in3), blocks_sent, extended.shape[1])
    stores = []
    for blocks, pairs in in_parts(links):
        values = relax(extended, couple, inverse, rhs, blocks, pairs, extended.shape[1])
        for block, value in zip(blocks, values):
            fresh[block] = value
            stores.append(
                pltpu.make_async_copy(fresh.at[block], traces.at[block], departures.at[block])
            )
            stores[block].start()
            column[pl.ds(block, 1), :] = value[0:1].astype(jnp.bfloat16).astype(jnp.float32)
    for start in range(0, cell_faces.shape[0], 8):
        index = cell_faces[pl.ds(start, 8), :]
        rows = range(column.shape[0])
        partial[pl.ds(start, 8), :] = look_up(
            column, 0, rows, index >> 7, index & (lane_width - 1), nothing()
        )
    for store in stores:
        store.wait()


def cells_kernel(
    mesh_dims, blocks, blocks_sent, partial, in1, in3, in0, in2, across,
    cell_faces, coeff, source, flags, sat, ratio, out, faces,
):
    places = sides_of(*mesh_dims)
    groups = sat.shape[0] // 4
    for (side, exists), came in zip(places, (in0, in1, in2, in3)):
        value = came[...].astype(jnp.float32)[0:blocks_sent]
        value = jnp.where(exists, value, jnp.zeros_like(value))
        for block in range(blocks_sent):
            faces[pl.ds(side * blocks_sent + block, 1), :] = value[block : block + 1]
    modes = [sat[pl.ds(mode, groups, stride=4), :] for mode in range(4)]
    weights = [coeff[pl.ds(face * groups, groups), :] for face in range(6)]
    traces = []
    for face in range(6):
        parts = []
        for start in range(0, groups, 8):
            rows = pl.ds(face * groups + start, 8)
            index = cell_faces[rows, :]
            high, low = (index >> 7) - blocks, index & (lane_width - 1)
            parts.append(look_up(faces, 0, range(4 * blocks_sent), high, low, partial[rows, :]))
        traces.append(jnp.concatenate(parts, 0))
    total = weights[0]
    gained = source[...] + weights[0] * traces[0]
    for face in range(1, 6):
        total = total + weights[face]
        gained = gained + weights[face] * traces[face]
    pressure = gained / total
    flux = [weights[face] * (pressure - traces[face]) for face in range(6)]
    flow = []
    for face in range(6):
        mode = modes[face // 2 + 1]
        own = modes[0] - mode if face % 2 == 0 else modes[0] + mode
        rows = pl.ds(face * groups, groups)
        flow.append(flux[face] * jnp.where(flags[rows, :] == 1, own, across[rows, :]))
    step = ratio[...]
    out[pl.ds(0, groups, stride=4), :] = modes[0] - step * (
        flow[0] + flow[1] + flow[2] + flow[3] + flow[4] + flow[5]
    )
    for mode in range(1, 4):
        lo, hi = 2 * mode - 2, 2 * mode - 1
        volume = 0.5 * (flux[hi] - flux[lo]) * modes[0]
        out[pl.ds(mode, groups, stride=4), :] = modes[mode] + 3.0 * step * (
            volume - (flow[hi] - flow[lo])
        )


whole = pl.BlockSpec(memory_space=pltpu.VMEM)
far = pl.BlockSpec(memory_space=pl.ANY)


def call(kernel, outs, specs, scratch=(), flops=0, traffic=0, out_specs=None, aliases=None):
    return pl.pallas_call(
        kernel,
        out_shape=outs,
        in_specs=specs,
        out_specs=[whole] * len(outs) if out_specs is None else out_specs,
        scratch_shapes=list(scratch),
        input_output_aliases=aliases or {},
        compiler_params=pltpu.CompilerParams(vmem_limit_bytes=vmem_bytes),
        cost_estimate=pl.CostEstimate(flops=flops, bytes_accessed=traffic, transcendentals=0),
    )


def keep_far(array):
    return pltpu.with_memory_space_constraint(array, pltpu.HBM)


def by_cells(array):
    return array.reshape(-1, lane_width)


def by_groups(array):
    rows = array.shape[0]
    return jnp.swapaxes(array.reshape(rows, -1, lane_width), 0, 1).reshape(-1, lane_width)


def per_device(
    mesh_dims,
    plans,
    trace_guess,
    trace_rhs,
    block_inverse,
    coupling,
    block_neighbours,
    block_send,
    cell_faces,
    face_coeff,
    cell_source,
    cell_neighbours,
    upwind_flags,
    cell_send,
    saturation,
    step_ratio,
):
    guess = trace_guess[0, 0]
    rhs = trace_rhs[0, 0]
    inverse = block_inverse[0, 0]
    couple = coupling[0, 0]
    links = block_neighbours[0, 0].T
    sends = block_send[0, 0].T
    blocks, columns, size = guess.shape
    blocks_sent = sends.shape[0]
    halo_rows = blocks_sent * columns
    extended_blocks = blocks + 4 * blocks_sent
    sat = by_groups(saturation[0, 0])
    cell_list = by_groups(cell_send[0, 0])
    halves = cell_list.shape[0] // 4
    groups = sat.shape[0] // 4
    half, single = jnp.bfloat16, jnp.float32

    def like(array):
        return jax.ShapeDtypeStruct(array.shape, array.dtype)

    widened = (extended_blocks, columns, size)
    *packed, guess = call(
        functools.partial(pack_kernel, mesh_dims),
        [jax.ShapeDtypeStruct((halo_rows + tail_rows, size), half)] * 4 + [like(guess)],
        [far] * 4,
        [
            pltpu.VMEM(sends.shape, jnp.int32),
            pltpu.VMEM(cell_list.shape, jnp.int32),
            pltpu.VMEM(sat.shape, single),
            pltpu.VMEM((4 * halves, lane_width), single),
            pltpu.SemaphoreType.DMA((3 + blocks,)),
        ],
    )(*map(keep_far, (sends, guess, cell_list, sat)))
    arrived = trade(packed, plans)

    remote = [
        couple,
        inverse,
        rhs,
        by_cells(cell_faces[0, 0]),
        by_cells(face_coeff[0, 0]),
        by_cells(cell_source[0]),
        by_cells(cell_neighbours[0, 0]),
        by_cells(upwind_flags[0, 0]),
        sat,
        by_cells(step_ratio[0]),
        links,
        sends,
    ]
    (
        couple,
        inverse,
        rhs,
        cell_faces,
        coeff,
        source,
        neighbours,
        flags,
        sat,
        ratio,
        links,
        _,
        near0,
        near1,
        extended,
        *listed,
    ) = call(
        functools.partial(fetch_kernel, mesh_dims, len(remote)),
        [like(array) for array in remote]
        + [like(sends)] * 2
        + [jax.ShapeDtypeStruct(widened, half)]
        + [
            jax.ShapeDtypeStruct((4 * blocks_sent,) + array.shape[1:], array.dtype)
            for array in remote[:3]
        ],
        [whole] + [far] * len(remote),
        [pltpu.SemaphoreType.DMA((len(remote),))],
        traffic=4 * guess.size,
    )(guess, *map(keep_far, remote))

    sweep_flops = 6 * blocks * columns * size * size
    extended, *packed = call(
        functools.partial(first_edge_kernel, mesh_dims),
        [like(extended)] + [jax.ShapeDtypeStruct((halo_rows, size), half)] * 4,
        [whole] * 10,
        flops=sweep_flops // 2,
        aliases={2: 0},
    )(near0, near1, extended, *(arrived[k] for k in (1, 0, 2, 3)), *listed)
    swept = trade(packed, plans)

    tails = [piece[halo_rows:] for piece in arrived]
    cell_rows = -(-(groups + halves) // 8) * 8
    extended, across = call(
        functools.partial(first_sweep_kernel, mesh_dims, halves),
        [like(extended), jax.ShapeDtypeStruct(neighbours.shape, single)],
        [whole] * 11,
        [pltpu.VMEM((6 * cell_rows, lane_width), single)],
        sweep_flops,
    )(links, extended, couple, inverse, rhs, sat, neighbours, *tails)

    extended, *packed = call(
        functools.partial(second_edge_kernel, mesh_dims),
        [like(extended)] + [jax.ShapeDtypeStruct((tail_rows, size), half)] * 4,
        [whole] * 10,
        flops=sweep_flops // 16,
        aliases={2: 0},
    )(near0, near1, extended, *(swept[k] for k in (1, 0, 2, 3)), *listed)
    edges = trade(packed, plans)

    traces, partial, _ = call(
        functools.partial(second_sweep_kernel, mesh_dims, blocks_sent),
        [
            jax.ShapeDtypeStruct(guess.shape, single),
            jax.ShapeDtypeStruct(coeff.shape, single),
            like(extended),
        ],
        [whole] * 10,
        [
            pltpu.VMEM(guess.shape, single),
            pltpu.VMEM((blocks, size), single),
            pltpu.SemaphoreType.DMA((blocks,)),
        ],
        sweep_flops,
        out_specs=[far, whole, whole],
        aliases={1: 2},
    )(links, extended, *swept, couple, inverse, rhs, cell_faces)

    (following,) = call(
        functools.partial(cells_kernel, mesh_dims, blocks, blocks_sent),
        [like(sat)],
        [whole] * 12,
        [pltpu.VMEM((4 * blocks_sent, lane_width), single)],
    )(partial, *(edges[k] for k in (1, 3, 0, 2)), across, cell_faces, coeff, source, flags, sat, ratio)
    saturation_next = jnp.swapaxes(following.reshape(groups, 4, lane_width), 0, 1).reshape(4, -1)
    return traces[None, None], saturation_next[None, None]


def solution(mesh):
    mesh_dims = (mesh.shape["wide"], mesh.shape["narrow"])

    def spec(rank):
        return P("wide", "narrow", *([None] * (rank - 2)))

    placed = tuple(spec(rank) for rank in (5, 5, 5, 6, 4, 4, 4, 4, 3, 4, 4, 4, 4, 3))
    return jax.shard_map(
        functools.partial(per_device, mesh_dims, pairings(*mesh_dims)),
        mesh=mesh,
        in_specs=placed,
        out_specs=(spec(5), spec(4)),
        check_vma=False,
    )
```

```python
import functools

import jax
import jax.numpy as jnp
from jax import lax
from jax.experimental import pallas as pl
from jax.experimental.pallas import tpu as pltpu
from jax.sharding import PartitionSpec as P

lane_width = 128
tail_rows = 16
vmem_bytes = 24 * 1024 * 1024
axes = ("wide", "narrow")


def pairings(wide, narrow):
    def number(i, j):
        return i * narrow + j

    def close(pairs, partner_of):
        taken = {d for pair in pairs for d in pair}
        for i in range(wide):
            for j in range(narrow):
                partner = partner_of(i, j)
                if number(i, j) in taken:
                    continue
                if 0 <= partner[0] < wide and 0 <= partner[1] < narrow:
                    if number(*partner) not in taken:
                        pairs.append((number(i, j), number(*partner)))
                        taken |= {number(i, j), number(*partner)}
        moves = [(a, b) for a, b in pairs] + [(b, a) for a, b in pairs if a != b]
        sources = {a for a, _ in moves}
        return moves + [(d, d) for d in range(wide * narrow) if d not in sources]

    plans = []
    for first in (0, 1):
        pairs = [
            (number(i, j), number(i + 1, j))
            for i in range(first, wide - 1, 2)
            for j in range(narrow)
        ]
        plans.append(close(pairs, lambda i, j: (i, j ^ 1)))
    for first in (0, 1):
        pairs = [
            (number(i, j), number(i, j + 1))
            for i in range(wide)
            for j in range(first, narrow - 1, 2)
        ]
        plans.append(close(pairs, lambda i, j: (i, narrow - 1 - j)))
    return plans


def trade(pieces, plans):
    return [lax.ppermute(piece, axes, plan) for piece, plan in zip(pieces, plans)]


def sides_of(wide, narrow):
    found = []
    for base, axis, count in ((0, "wide", wide), (2, "narrow", narrow)):
        here = lax.axis_index(axis)
        for first in (0, 1):
            partner = ((here + first) ^ 1) - first
            side = base + jnp.where(partner > here, 1, 0)
            found.append((side, (partner >= 0) & (partner < count)))
    return found


def spread(row):
    return jnp.broadcast_to(row, (8, lane_width))


def take_lanes(row, low):
    return jnp.take_along_axis(row, low, axis=1, mode="promise_in_bounds")


def pack_kernel(
    mesh_dims, sends_far, guess_far, list_far, sat_far,
    out0, out1, out2, out3, guess, sends,
    cell_list, sat, picked, arrivals,
):
    places = sides_of(*mesh_dims)
    blocks, size = guess.shape[0], guess.shape[1]
    copies = [
        pltpu.make_async_copy(far, near, arrivals.at[slot])
        for slot, (far, near) in enumerate(
            ((list_far, cell_list), (sat_far, sat), (sends_far, sends))
        )
    ]
    loads = [
        pltpu.make_async_copy(guess_far.at[block], guess.at[block], arrivals.at[3 + block])
        for block in range(blocks)
    ]
    for copy in copies + loads:
        copy.start()
    for copy in copies:
        copy.wait()
    blocks_sent = sends.shape[0]
    groups = sat.shape[0] // 4
    lists = cell_list.shape[0]
    halves = lists // 4
    index = cell_list[...]
    high = index >> 7
    low = index & (lane_width - 1)
    found = jnp.zeros(index.shape, jnp.float32)
    for group in range(groups):
        modes = sat[pl.ds(group * 4, 4), :]
        mean, along_x, along_y = modes[0:1], modes[1:2], modes[2:3]
        four = jnp.concatenate([mean - along_x, mean + along_x, mean - along_y, mean + along_y], 0)
        rows = jnp.concatenate([four] * halves, 0)
        found = jnp.where(high == group, take_lanes(rows, low), found)
    picked[...] = found
    for (side, _), out in zip(places, (out0, out1, out2, out3)):
        values = [picked[pl.ds(half * 4 + side, 1), :] for half in range(halves)]
        coarse = [value.astype(jnp.bfloat16).astype(jnp.float32) for value in values]
        fine = [value - rounded for value, rounded in zip(values, coarse)]
        blank = jnp.zeros((tail_rows - 2 * halves, lane_width), jnp.float32)
        out[pl.ds(blocks_sent * size, tail_rows), :] = jnp.concatenate(
            coarse + fine + [blank], 0
        ).astype(jnp.bfloat16)
    listed = listed_blocks(sends, places)
    for load in loads:
        load.wait()
    for picks, out in zip(listed, (out0, out1, out2, out3)):
        for slot, block in enumerate(picks):
            out[pl.ds(slot * size, size), :] = guess[block].astype(jnp.bfloat16)


def listed_blocks(sends, places):
    value = sends[...]
    count = value.shape[0]
    sides = [[value[slot, side] for slot in range(count)] for side in range(4)]
    found = []
    for pairing, (side, _) in enumerate(places):
        first = 0 if pairing < 2 else 2
        found.append(
            [jnp.where(side == first, a, b) for a, b in zip(sides[first], sides[first + 1])]
        )
    return found


def listed_links(near0, near1):
    values = near0[...], near1[...]
    slots, pairings = values[0].shape
    return [
        [value[slot, pairing] for value in values]
        for pairing in range(pairings)
        for slot in range(slots)
    ]


def linked_blocks(links):
    value = links[...]
    return [[value[k, block] for k in range(2)] for block in range(value.shape[1])]


def in_parts(links):
    pairs = linked_blocks(links)
    for start in range(0, len(pairs), 8):
        yield range(start, min(start + 8, len(pairs))), pairs[start : start + 8]


def fetch_kernel(mesh_dims, count, guess, sends, rhs_far, *refs):
    fars, nears = refs[:count], refs[count : 2 * count]
    near0, near1, extended, couple_listed, inverse_listed, rhs_listed, arrivals = refs[2 * count :]
    listed = sends[...]
    columns = []
    for pairing, (side, _) in enumerate(sides_of(*mesh_dims)):
        first = 0 if pairing < 2 else 2
        columns.append(
            jnp.where(side == first, listed[:, first : first + 1], listed[:, first + 1 : first + 2])
        )
    listed = jnp.concatenate(columns, 1)
    slots, pairings = listed.shape
    blocks = [listed[slot, pairing] for pairing in range(pairings) for slot in range(slots)]
    copies = [
        pltpu.make_async_copy(far, near, arrivals.at[slot])
        for slot, (far, near) in enumerate(zip(fars, nears))
    ] + [
        pltpu.make_async_copy(rhs_far.at[block], rhs_listed.at[place], arrivals.at[count + place])
        for place, block in enumerate(blocks)
    ]
    for copy in copies:
        copy.start()
    for block in range(guess.shape[0]):
        extended[block] = guess[block].astype(jnp.bfloat16)
    for copy in copies:
        copy.wait()
    couple, inverse, links = nears[0], nears[1], nears[-1][...]
    for place, block in enumerate(blocks):
        couple_listed[place] = couple[block]
        inverse_listed[place] = inverse[block]
    for k, near in enumerate((near0, near1)):
        chosen = jnp.zeros_like(listed)
        for block in range(links.shape[1]):
            chosen = jnp.where(listed == block, links[k, block], chosen)
        near[...] = chosen


def product(left, right):
    return lax.dot_general(
        left, right, (((1,), (1,)), ((), ())), preferred_element_type=jnp.float32
    )


def relax(extended, couple, inverse, rhs, blocks, links, rows):
    resid = []
    for block, pair in zip(blocks, links):
        near = jnp.concatenate([extended[link, 0:rows, :] for link in pair], 1)
        matrix = jnp.concatenate([couple[block, k] for k in range(len(pair))], 1)
        resid.append((rhs[block, 0:rows, :] - product(near, matrix)).astype(jnp.bfloat16))
    return [product(part, inverse[block]) for part, block in zip(resid, blocks)]


def land(extended, places, arrived, blocks_sent, rows):
    own_count = extended.shape[0] - 4 * blocks_sent
    size = extended.shape[1]
    for (side, exists), came in zip(places, arrived):
        for block in range(blocks_sent):
            value = came[pl.ds(block * size, rows), :]
            value = jnp.where(exists, value, jnp.zeros_like(value))
            extended[own_count + side * blocks_sent + block, 0:rows, :] = value


def first_edge_kernel(
    mesh_dims, near0, near1, _, in1, in0, in2, in3, couple, inverse, rhs,
    extended, out0, out1, out2, out3,
):
    size = extended.shape[1]
    slots = near0.shape[0]
    links = listed_links(near0, near1)
    land(extended, sides_of(*mesh_dims), (in0, in1, in2, in3), slots, size)
    fresh = relax(extended, couple, inverse, rhs, range(len(links)), links, size)
    for pairing, out in enumerate((out0, out1, out2, out3)):
        for slot in range(slots):
            value = fresh[pairing * slots + slot]
            out[pl.ds(slot * size, size), :] = value.astype(jnp.bfloat16)


def spread_rows(table, first_row, count):
    return [spread(table[pl.ds(first_row + row, 1), :]) for row in range(count)]


def look_up(rows, high, low, value):
    for number, row in enumerate(rows):
        value = jnp.where(high == number, take_lanes(row, low), value)
    return value


def nothing():
    return jnp.zeros((8, lane_width), jnp.float32)


def first_sweep_kernel(
    mesh_dims, halves, links, extended, couple, inverse, rhs,
    sat, neighbours, tail0, tail1, tail2, tail3,
    smoothed, across, across_rows,
):
    places = sides_of(*mesh_dims)
    groups = sat.shape[0] // 4
    stride = across_rows.shape[0] // 6
    modes = [sat[pl.ds(mode, groups, stride=4), :] for mode in range(4)]
    for (side, exists), came in zip(places, (tail0, tail1, tail2, tail3)):
        value = came[...].astype(jnp.float32)
        value = value[0:halves] + value[halves : 2 * halves]
        value = jnp.where(exists, value, jnp.zeros_like(value))
        for half in range(halves):
            across_rows[pl.ds(side * stride + groups + half, 1), :] = value[half : half + 1]
    for face in range(6):
        mode = modes[face // 2 + 1]
        across_rows[pl.ds(face * stride, groups), :] = (
            modes[0] + mode if face % 2 == 0 else modes[0] - mode
        )
    for face in range(6):
        rows = spread_rows(across_rows, face * stride, groups + halves if face < 4 else groups)
        for start in range(0, groups, 8):
            index = neighbours[pl.ds(face * groups + start, 8), :]
            high, low = index >> 7, index & (lane_width - 1)
            if 0 < face < 4:
                high = jnp.where(high >= groups, high - face * halves, high)
            across[pl.ds(face * groups + start, 8), :] = look_up(rows, high, low, nothing())
    for blocks, pairs in in_parts(links):
        fresh = relax(extended, couple, inverse, rhs, blocks, pairs, extended.shape[1])
        for block, value in zip(blocks, fresh):
            smoothed[block] = value.astype(jnp.bfloat16)


def second_edge_kernel(
    mesh_dims, near0, near1, _, in1, in0, in2, in3, couple, inverse, rhs,
    extended, out0, out1, out2, out3,
):
    slots = near0.shape[0]
    links = listed_links(near0, near1)
    land(extended, sides_of(*mesh_dims), (in0, in1, in2, in3), slots, tail_rows)
    fresh = relax(extended, couple, inverse, rhs, range(len(links)), links, tail_rows)
    for pairing, out in enumerate((out0, out1, out2, out3)):
        rows = [fresh[pairing * slots + slot][0:1, :] for slot in range(slots)]
        blank = jnp.zeros((tail_rows - len(rows), lane_width), jnp.float32)
        out[...] = jnp.concatenate(rows + [blank], 0).astype(jnp.bfloat16)


def second_sweep_kernel(
    mesh_dims, blocks_sent, links, _, in0, in1, in2, in3, couple, inverse, rhs, cell_faces,
    traces, partial, extended, fresh, column, departures,
):
    land(extended, sides_of(*mesh_dims), (in0, in1, in2, in3), blocks_sent, extended.shape[1])
    stores = []
    for blocks, pairs in in_parts(links):
        values = relax(extended, couple, inverse, rhs, blocks, pairs, extended.shape[1])
        for block, value in zip(blocks, values):
            fresh[block] = value
            stores.append(
                pltpu.make_async_copy(fresh.at[block], traces.at[block], departures.at[block])
            )
            stores[block].start()
            column[pl.ds(block, 1), :] = value[0:1].astype(jnp.bfloat16).astype(jnp.float32)
    rows = spread_rows(column, 0, column.shape[0])
    for start in range(0, cell_faces.shape[0], 8):
        index = cell_faces[pl.ds(start, 8), :]
        partial[pl.ds(start, 8), :] = look_up(
            rows, index >> 7, index & (lane_width - 1), nothing()
        )
    for store in stores:
        store.wait()


def cells_kernel(
    mesh_dims, blocks, blocks_sent, partial, in1, in3, in0, in2, across,
    cell_faces, coeff, source, flags, sat, ratio, out, faces,
):
    places = sides_of(*mesh_dims)
    groups = sat.shape[0] // 4
    for (side, exists), came in zip(places, (in0, in1, in2, in3)):
        value = came[...].astype(jnp.float32)[0:blocks_sent]
        value = jnp.where(exists, value, jnp.zeros_like(value))
        for block in range(blocks_sent):
            faces[pl.ds(side * blocks_sent + block, 1), :] = value[block : block + 1]
    modes = [sat[pl.ds(mode, groups, stride=4), :] for mode in range(4)]
    weights = [coeff[pl.ds(face * groups, groups), :] for face in range(6)]
    edge_rows = spread_rows(faces, 0, 4 * blocks_sent)
    traces = []
    for face in range(6):
        parts = []
        for start in range(0, groups, 8):
            rows = pl.ds(face * groups + start, 8)
            index = cell_faces[rows, :]
            high, low = (index >> 7) - blocks, index & (lane_width - 1)
            parts.append(look_up(edge_rows, high, low, partial[rows, :]))
        traces.append(jnp.concatenate(parts, 0))
    total = weights[0]
    gained = source[...] + weights[0] * traces[0]
    for face in range(1, 6):
        total = total + weights[face]
        gained = gained + weights[face] * traces[face]
    pressure = gained / total
    flux = [weights[face] * (pressure - traces[face]) for face in range(6)]
    flow = []
    for face in range(6):
        mode = modes[face // 2 + 1]
        own = modes[0] - mode if face % 2 == 0 else modes[0] + mode
        rows = pl.ds(face * groups, groups)
        flow.append(flux[face] * jnp.where(flags[rows, :] == 1, own, across[rows, :]))
    step = ratio[...]
    out[pl.ds(0, groups, stride=4), :] = modes[0] - step * (
        flow[0] + flow[1] + flow[2] + flow[3] + flow[4] + flow[5]
    )
    for mode in range(1, 4):
        lo, hi = 2 * mode - 2, 2 * mode - 1
        volume = 0.5 * (flux[hi] - flux[lo]) * modes[0]
        out[pl.ds(mode, groups, stride=4), :] = modes[mode] + 3.0 * step * (
            volume - (flow[hi] - flow[lo])
        )


whole = pl.BlockSpec(memory_space=pltpu.VMEM)
far = pl.BlockSpec(memory_space=pl.ANY)


def call(kernel, outs, specs, scratch=(), flops=0, traffic=0, out_specs=None, aliases=None):
    return pl.pallas_call(
        kernel,
        out_shape=outs,
        in_specs=specs,
        out_specs=[whole] * len(outs) if out_specs is None else out_specs,
        scratch_shapes=list(scratch),
        input_output_aliases=aliases or {},
        compiler_params=pltpu.CompilerParams(vmem_limit_bytes=vmem_bytes),
        cost_estimate=pl.CostEstimate(flops=flops, bytes_accessed=traffic, transcendentals=0),
    )


def keep_far(array):
    return pltpu.with_memory_space_constraint(array, pltpu.HBM)


def by_cells(array):
    return array.reshape(-1, lane_width)


def by_groups(array):
    rows = array.shape[0]
    return jnp.swapaxes(array.reshape(rows, -1, lane_width), 0, 1).reshape(-1, lane_width)


def per_device(
    mesh_dims,
    plans,
    trace_guess,
    trace_rhs,
    block_inverse,
    coupling,
    block_neighbours,
    block_send,
    cell_faces,
    face_coeff,
    cell_source,
    cell_neighbours,
    upwind_flags,
    cell_send,
    saturation,
    step_ratio,
):
    guess = trace_guess[0, 0]
    rhs = trace_rhs[0, 0]
    inverse = block_inverse[0, 0]
    couple = coupling[0, 0]
    links = block_neighbours[0, 0].T
    sends = block_send[0, 0].T
    blocks, columns, size = guess.shape
    blocks_sent = sends.shape[0]
    halo_rows = blocks_sent * columns
    extended_blocks = blocks + 4 * blocks_sent
    sat = by_groups(saturation[0, 0])
    cell_list = by_groups(cell_send[0, 0])
    halves = cell_list.shape[0] // 4
    groups = sat.shape[0] // 4
    half, single = jnp.bfloat16, jnp.float32

    def like(array):
        return jax.ShapeDtypeStruct(array.shape, array.dtype)

    widened = (extended_blocks, columns, size)
    *packed, guess, sends = call(
        functools.partial(pack_kernel, mesh_dims),
        [jax.ShapeDtypeStruct((halo_rows + tail_rows, size), half)] * 4
        + [like(guess), like(sends)],
        [far] * 4,
        [
            pltpu.VMEM(cell_list.shape, jnp.int32),
            pltpu.VMEM(sat.shape, single),
            pltpu.VMEM((4 * halves, lane_width), single),
            pltpu.SemaphoreType.DMA((3 + blocks,)),
        ],
    )(*map(keep_far, (sends, guess, cell_list, sat)))
    arrived = trade(packed, plans)

    remote = [
        couple,
        inverse,
        by_cells(cell_faces[0, 0]),
        by_cells(face_coeff[0, 0]),
        by_cells(cell_source[0]),
        by_cells(cell_neighbours[0, 0]),
        by_cells(upwind_flags[0, 0]),
        sat,
        by_cells(step_ratio[0]),
        links,
    ]
    (
        couple,
        inverse,
        cell_faces,
        coeff,
        source,
        neighbours,
        flags,
        sat,
        ratio,
        links,
        near0,
        near1,
        extended,
        *listed,
    ) = call(
        functools.partial(fetch_kernel, mesh_dims, len(remote)),
        [like(array) for array in remote]
        + [like(sends)] * 2
        + [jax.ShapeDtypeStruct(widened, half)]
        + [
            jax.ShapeDtypeStruct((4 * blocks_sent,) + array.shape[1:], array.dtype)
            for array in (couple, inverse, rhs)
        ],
        [whole, whole] + [far] * (1 + len(remote)),
        [pltpu.SemaphoreType.DMA((len(remote) + 4 * blocks_sent,))],
        traffic=4 * guess.size,
    )(guess, sends, *map(keep_far, [rhs] + remote))

    sweep_flops = 6 * blocks * columns * size * size
    extended, *packed = call(
        functools.partial(first_edge_kernel, mesh_dims),
        [like(extended)] + [jax.ShapeDtypeStruct((halo_rows, size), half)] * 4,
        [whole] * 10,
        flops=sweep_flops // 2,
        aliases={2: 0},
    )(near0, near1, extended, *(arrived[k] for k in (1, 0, 2, 3)), *listed)
    swept = trade(packed, plans)

    tails = [piece[halo_rows:] for piece in arrived]
    cell_rows = -(-(groups + halves) // 8) * 8
    extended, across = call(
        functools.partial(first_sweep_kernel, mesh_dims, halves),
        [like(extended), jax.ShapeDtypeStruct(neighbours.shape, single)],
        [whole] * 11,
        [pltpu.VMEM((6 * cell_rows, lane_width), single)],
        sweep_flops,
    )(links, extended, couple, inverse, rhs, sat, neighbours, *tails)

    extended, *packed = call(
        functools.partial(second_edge_kernel, mesh_dims),
        [like(extended)] + [jax.ShapeDtypeStruct((tail_rows, size), half)] * 4,
        [whole] * 10,
        flops=sweep_flops // 16,
        aliases={2: 0},
    )(near0, near1, extended, *(swept[k] for k in (1, 0, 2, 3)), *listed)
    edges = trade(packed, plans)

    traces, partial, _ = call(
        functools.partial(second_sweep_kernel, mesh_dims, blocks_sent),
        [
            jax.ShapeDtypeStruct(guess.shape, single),
            jax.ShapeDtypeStruct(coeff.shape, single),
            like(extended),
        ],
        [whole] * 10,
        [
            pltpu.VMEM(guess.shape, single),
            pltpu.VMEM((blocks, size), single),
            pltpu.SemaphoreType.DMA((blocks,)),
        ],
        sweep_flops,
        out_specs=[far, whole, whole],
        aliases={1: 2},
    )(links, extended, *swept, couple, inverse, rhs, cell_faces)

    (following,) = call(
        functools.partial(cells_kernel, mesh_dims, blocks, blocks_sent),
        [like(sat)],
        [whole] * 12,
        [pltpu.VMEM((4 * blocks_sent, lane_width), single)],
    )(partial, *(edges[k] for k in (1, 3, 0, 2)), across, cell_faces, coeff, source, flags, sat, ratio)
    saturation_next = jnp.swapaxes(following.reshape(groups, 4, lane_width), 0, 1).reshape(4, -1)
    return traces[None, None], saturation_next[None, None]


def solution(mesh):
    mesh_dims = (mesh.shape["wide"], mesh.shape["narrow"])

    def spec(rank):
        return P("wide", "narrow", *([None] * (rank - 2)))

    placed = tuple(spec(rank) for rank in (5, 5, 5, 6, 4, 4, 4, 4, 3, 4, 4, 4, 4, 3))
    return jax.shard_map(
        functools.partial(per_device, mesh_dims, pairings(*mesh_dims)),
        mesh=mesh,
        in_specs=placed,
        out_specs=(spec(5), spec(4)),
        check_vma=False,
    )
```

```python
import functools

import jax
import jax.numpy as jnp
from jax import lax
from jax.experimental import pallas as pl
from jax.experimental.pallas import tpu as pltpu
from jax.sharding import PartitionSpec as P

lane_width = 128
tail_rows = 16
vmem_bytes = 24 * 1024 * 1024
axes = ("wide", "narrow")


def pairings(wide, narrow):
    def number(i, j):
        return i * narrow + j

    def close(pairs, partner_of):
        taken = {d for pair in pairs for d in pair}
        for i in range(wide):
            for j in range(narrow):
                partner = partner_of(i, j)
                if number(i, j) in taken:
                    continue
                if 0 <= partner[0] < wide and 0 <= partner[1] < narrow:
                    if number(*partner) not in taken:
                        pairs.append((number(i, j), number(*partner)))
                        taken |= {number(i, j), number(*partner)}
        moves = [(a, b) for a, b in pairs] + [(b, a) for a, b in pairs if a != b]
        sources = {a for a, _ in moves}
        return moves + [(d, d) for d in range(wide * narrow) if d not in sources]

    plans = []
    for first in (0, 1):
        pairs = [
            (number(i, j), number(i + 1, j))
            for i in range(first, wide - 1, 2)
            for j in range(narrow)
        ]
        plans.append(close(pairs, lambda i, j: (i, j ^ 1)))
    for first in (0, 1):
        pairs = [
            (number(i, j), number(i, j + 1))
            for i in range(wide)
            for j in range(first, narrow - 1, 2)
        ]
        plans.append(close(pairs, lambda i, j: (i, narrow - 1 - j)))
    return plans


def trade(pieces, plans):
    return [lax.ppermute(piece, axes, plan) for piece, plan in zip(pieces, plans)]


def sides_of(wide, narrow):
    found = []
    for base, axis, count in ((0, "wide", wide), (2, "narrow", narrow)):
        here = lax.axis_index(axis)
        for first in (0, 1):
            partner = ((here + first) ^ 1) - first
            side = base + jnp.where(partner > here, 1, 0)
            found.append((side, (partner >= 0) & (partner < count)))
    return found


def spread(row):
    return jnp.broadcast_to(row, (8, lane_width))


def take_lanes(row, low):
    return jnp.take_along_axis(row, low, axis=1, mode="promise_in_bounds")


def pack_kernel(
    mesh_dims, sends_far, guess_far, list_far, sat_far,
    out0, out1, out2, out3, guess, sends,
    cell_list, sat, picked, arrivals,
):
    places = sides_of(*mesh_dims)
    blocks, size = guess.shape[0], guess.shape[1]
    copies = [
        pltpu.make_async_copy(far, near, arrivals.at[slot])
        for slot, (far, near) in enumerate(
            ((list_far, cell_list), (sat_far, sat), (sends_far, sends))
        )
    ]
    loads = [
        pltpu.make_async_copy(guess_far.at[block], guess.at[block], arrivals.at[3 + block])
        for block in range(blocks)
    ]
    for copy in copies + loads:
        copy.start()
    for copy in copies:
        copy.wait()
    blocks_sent = sends.shape[0]
    groups = sat.shape[0] // 4
    lists = cell_list.shape[0]
    halves = lists // 4
    index = cell_list[...]
    high = index >> 7
    low = index & (lane_width - 1)
    found = jnp.zeros(index.shape, jnp.float32)
    for group in range(groups):
        modes = sat[pl.ds(group * 4, 4), :]
        mean, along_x, along_y = modes[0:1], modes[1:2], modes[2:3]
        four = jnp.concatenate([mean - along_x, mean + along_x, mean - along_y, mean + along_y], 0)
        rows = jnp.concatenate([four] * halves, 0)
        found = jnp.where(high == group, take_lanes(rows, low), found)
    picked[...] = found
    for (side, _), out in zip(places, (out0, out1, out2, out3)):
        values = [picked[pl.ds(half * 4 + side, 1), :] for half in range(halves)]
        coarse = [value.astype(jnp.bfloat16).astype(jnp.float32) for value in values]
        fine = [value - rounded for value, rounded in zip(values, coarse)]
        blank = jnp.zeros((tail_rows - 2 * halves, lane_width), jnp.float32)
        out[pl.ds(blocks_sent * size, tail_rows), :] = jnp.concatenate(
            coarse + fine + [blank], 0
        ).astype(jnp.bfloat16)
    listed = listed_blocks(sends, places)
    for load in loads:
        load.wait()
    for picks, out in zip(listed, (out0, out1, out2, out3)):
        for slot, block in enumerate(picks):
            out[pl.ds(slot * size, size), :] = guess[block].astype(jnp.bfloat16)


def listed_blocks(sends, places):
    value = sends[...]
    count = value.shape[0]
    sides = [[value[slot, side] for slot in range(count)] for side in range(4)]
    found = []
    for pairing, (side, _) in enumerate(places):
        first = 0 if pairing < 2 else 2
        found.append(
            [jnp.where(side == first, a, b) for a, b in zip(sides[first], sides[first + 1])]
        )
    return found


def listed_links(near0, near1):
    values = near0[...], near1[...]
    slots, pairings = values[0].shape
    return [
        [value[slot, pairing] for value in values]
        for pairing in range(pairings)
        for slot in range(slots)
    ]


def linked_blocks(links):
    value = links[...]
    return [[value[k, block] for k in range(2)] for block in range(value.shape[1])]


def in_parts(links):
    pairs = linked_blocks(links)
    for start in range(0, len(pairs), 8):
        yield range(start, min(start + 8, len(pairs))), pairs[start : start + 8]


def fetch_kernel(mesh_dims, count, guess, sends, rhs_far, *refs):
    fars, nears = refs[:count], refs[count : 2 * count]
    near0, near1, own, couple_listed, inverse_listed, rhs_listed, arrivals = refs[2 * count :]
    listed = sends[...]
    columns = []
    for pairing, (side, _) in enumerate(sides_of(*mesh_dims)):
        first = 0 if pairing < 2 else 2
        columns.append(
            jnp.where(side == first, listed[:, first : first + 1], listed[:, first + 1 : first + 2])
        )
    listed = jnp.concatenate(columns, 1)
    slots, pairings = listed.shape
    blocks = [listed[slot, pairing] for pairing in range(pairings) for slot in range(slots)]
    copies = [
        pltpu.make_async_copy(far, near, arrivals.at[slot])
        for slot, (far, near) in enumerate(zip(fars, nears))
    ] + [
        pltpu.make_async_copy(rhs_far.at[block], rhs_listed.at[place], arrivals.at[count + place])
        for place, block in enumerate(blocks)
    ]
    for copy in copies:
        copy.start()
    for block in range(guess.shape[0]):
        own[block] = guess[block].astype(jnp.bfloat16)
    for copy in copies:
        copy.wait()
    couple, inverse, links = nears[0], nears[1], nears[-1][...]
    for place, block in enumerate(blocks):
        couple_listed[place] = couple[block]
        inverse_listed[place] = inverse[block]
    for k, near in enumerate((near0, near1)):
        chosen = jnp.zeros_like(listed)
        for block in range(links.shape[1]):
            chosen = jnp.where(listed == block, links[k, block], chosen)
        near[...] = chosen


def product(left, right):
    return lax.dot_general(
        left, right, (((1,), (1,)), ((), ())), preferred_element_type=jnp.float32
    )


def relax(extended, couple, inverse, rhs, blocks, links, rows):
    resid = []
    for block, pair in zip(blocks, links):
        near = jnp.concatenate([extended[link, 0:rows, :] for link in pair], 1)
        matrix = jnp.concatenate([couple[block, k] for k in range(len(pair))], 1)
        resid.append((rhs[block, 0:rows, :] - product(near, matrix)).astype(jnp.bfloat16))
    return [product(part, inverse[block]) for part, block in zip(resid, blocks)]


def extend(extended, own, places, arrived, blocks_sent):
    own_count, size = own.shape[:2]
    rows = extended.shape[1]
    for block in range(own_count):
        extended[block] = own[block, 0:rows, :]
    for (side, exists), came in zip(places, arrived):
        for block in range(blocks_sent):
            value = came[pl.ds(block * size, rows), :]
            value = jnp.where(exists, value, jnp.zeros_like(value))
            extended[own_count + side * blocks_sent + block] = value


def first_edge_kernel(
    mesh_dims, near0, near1, own, in1, in0, in2, in3, couple, inverse, rhs,
    extended, out0, out1, out2, out3,
):
    size = extended.shape[1]
    slots = near0.shape[0]
    links = listed_links(near0, near1)
    extend(extended, own, sides_of(*mesh_dims), (in0, in1, in2, in3), slots)
    fresh = relax(extended, couple, inverse, rhs, range(len(links)), links, size)
    for pairing, out in enumerate((out0, out1, out2, out3)):
        for slot in range(slots):
            value = fresh[pairing * slots + slot]
            out[pl.ds(slot * size, size), :] = value.astype(jnp.bfloat16)


def spread_rows(table, first_row, count):
    return [spread(table[pl.ds(first_row + row, 1), :]) for row in range(count)]


def look_up(rows, high, low, value):
    for number, row in enumerate(rows):
        value = jnp.where(high == number, take_lanes(row, low), value)
    return value


def nothing():
    return jnp.zeros((8, lane_width), jnp.float32)


def first_sweep_kernel(
    mesh_dims, halves, links, extended, couple, inverse, rhs,
    sat, neighbours, tail0, tail1, tail2, tail3,
    smoothed, across, across_rows,
):
    places = sides_of(*mesh_dims)
    groups = sat.shape[0] // 4
    stride = across_rows.shape[0] // 6
    modes = [sat[pl.ds(mode, groups, stride=4), :] for mode in range(4)]
    for (side, exists), came in zip(places, (tail0, tail1, tail2, tail3)):
        value = came[...].astype(jnp.float32)
        value = value[0:halves] + value[halves : 2 * halves]
        value = jnp.where(exists, value, jnp.zeros_like(value))
        for half in range(halves):
            across_rows[pl.ds(side * stride + groups + half, 1), :] = value[half : half + 1]
    for face in range(6):
        mode = modes[face // 2 + 1]
        across_rows[pl.ds(face * stride, groups), :] = (
            modes[0] + mode if face % 2 == 0 else modes[0] - mode
        )
    for face in range(6):
        rows = spread_rows(across_rows, face * stride, groups + halves if face < 4 else groups)
        for start in range(0, groups, 8):
            index = neighbours[pl.ds(face * groups + start, 8), :]
            high, low = index >> 7, index & (lane_width - 1)
            if 0 < face < 4:
                high = jnp.where(high >= groups, high - face * halves, high)
            across[pl.ds(face * groups + start, 8), :] = look_up(rows, high, low, nothing())
    for blocks, pairs in in_parts(links):
        fresh = relax(extended, couple, inverse, rhs, blocks, pairs, extended.shape[1])
        for block, value in zip(blocks, fresh):
            smoothed[block] = value.astype(jnp.bfloat16)


def second_edge_kernel(
    mesh_dims, near0, near1, own, in1, in0, in2, in3, couple, inverse, rhs,
    out0, out1, out2, out3, extended,
):
    slots = near0.shape[0]
    links = listed_links(near0, near1)
    extend(extended, own, sides_of(*mesh_dims), (in0, in1, in2, in3), slots)
    fresh = relax(extended, couple, inverse, rhs, range(len(links)), links, tail_rows)
    for pairing, out in enumerate((out0, out1, out2, out3)):
        rows = [fresh[pairing * slots + slot][0:1, :] for slot in range(slots)]
        blank = jnp.zeros((tail_rows - len(rows), lane_width), jnp.float32)
        out[...] = jnp.concatenate(rows + [blank], 0).astype(jnp.bfloat16)


def second_sweep_kernel(
    mesh_dims, blocks_sent, links, own, in1, in0, in2, in3, couple, inverse, rhs, cell_faces,
    traces, partial, extended, fresh, column, departures,
):
    extend(extended, own, sides_of(*mesh_dims), (in0, in1, in2, in3), blocks_sent)
    stores = []
    for blocks, pairs in in_parts(links):
        values = relax(extended, couple, inverse, rhs, blocks, pairs, extended.shape[1])
        for block, value in zip(blocks, values):
            fresh[block] = value
            stores.append(
                pltpu.make_async_copy(fresh.at[block], traces.at[block], departures.at[block])
            )
            stores[block].start()
            column[pl.ds(block, 1), :] = value[0:1].astype(jnp.bfloat16).astype(jnp.float32)
    rows = spread_rows(column, 0, column.shape[0])
    for start in range(0, cell_faces.shape[0], 8):
        index = cell_faces[pl.ds(start, 8), :]
        partial[pl.ds(start, 8), :] = look_up(
            rows, index >> 7, index & (lane_width - 1), nothing()
        )
    for store in stores:
        store.wait()


def cells_kernel(
    mesh_dims, blocks, blocks_sent, partial, in1, in3, in0, in2, across,
    cell_faces, coeff, source, flags, sat, ratio, out, faces,
):
    places = sides_of(*mesh_dims)
    groups = sat.shape[0] // 4
    for (side, exists), came in zip(places, (in0, in1, in2, in3)):
        value = came[...].astype(jnp.float32)[0:blocks_sent]
        value = jnp.where(exists, value, jnp.zeros_like(value))
        for block in range(blocks_sent):
            faces[pl.ds(side * blocks_sent + block, 1), :] = value[block : block + 1]
    modes = [sat[pl.ds(mode, groups, stride=4), :] for mode in range(4)]
    weights = [coeff[pl.ds(face * groups, groups), :] for face in range(6)]
    edge_rows = spread_rows(faces, 0, 4 * blocks_sent)
    traces = []
    for face in range(6):
        parts = []
        for start in range(0, groups, 8):
            rows = pl.ds(face * groups + start, 8)
            index = cell_faces[rows, :]
            high, low = (index >> 7) - blocks, index & (lane_width - 1)
            parts.append(look_up(edge_rows, high, low, partial[rows, :]))
        traces.append(jnp.concatenate(parts, 0))
    total = weights[0]
    gained = source[...] + weights[0] * traces[0]
    for face in range(1, 6):
        total = total + weights[face]
        gained = gained + weights[face] * traces[face]
    pressure = gained / total
    flux = [weights[face] * (pressure - traces[face]) for face in range(6)]
    flow = []
    for face in range(6):
        mode = modes[face // 2 + 1]
        own = modes[0] - mode if face % 2 == 0 else modes[0] + mode
        rows = pl.ds(face * groups, groups)
        flow.append(flux[face] * jnp.where(flags[rows, :] == 1, own, across[rows, :]))
    step = ratio[...]
    out[pl.ds(0, groups, stride=4), :] = modes[0] - step * (
        flow[0] + flow[1] + flow[2] + flow[3] + flow[4] + flow[5]
    )
    for mode in range(1, 4):
        lo, hi = 2 * mode - 2, 2 * mode - 1
        volume = 0.5 * (flux[hi] - flux[lo]) * modes[0]
        out[pl.ds(mode, groups, stride=4), :] = modes[mode] + 3.0 * step * (
            volume - (flow[hi] - flow[lo])
        )


whole = pl.BlockSpec(memory_space=pltpu.VMEM)
far = pl.BlockSpec(memory_space=pl.ANY)


def call(kernel, outs, specs, scratch=(), flops=0, traffic=0, out_specs=None):
    return pl.pallas_call(
        kernel,
        out_shape=outs,
        in_specs=specs,
        out_specs=[whole] * len(outs) if out_specs is None else out_specs,
        scratch_shapes=list(scratch),
        compiler_params=pltpu.CompilerParams(vmem_limit_bytes=vmem_bytes),
        cost_estimate=pl.CostEstimate(flops=flops, bytes_accessed=traffic, transcendentals=0),
    )


def keep_far(array):
    return pltpu.with_memory_space_constraint(array, pltpu.HBM)


def by_cells(array):
    return array.reshape(-1, lane_width)


def by_groups(array):
    rows = array.shape[0]
    return jnp.swapaxes(array.reshape(rows, -1, lane_width), 0, 1).reshape(-1, lane_width)


def per_device(
    mesh_dims,
    plans,
    trace_guess,
    trace_rhs,
    block_inverse,
    coupling,
    block_neighbours,
    block_send,
    cell_faces,
    face_coeff,
    cell_source,
    cell_neighbours,
    upwind_flags,
    cell_send,
    saturation,
    step_ratio,
):
    guess = trace_guess[0, 0]
    rhs = trace_rhs[0, 0]
    inverse = block_inverse[0, 0]
    couple = coupling[0, 0]
    links = block_neighbours[0, 0].T
    sends = block_send[0, 0].T
    blocks, columns, size = guess.shape
    blocks_sent = sends.shape[0]
    halo_rows = blocks_sent * columns
    extended_blocks = blocks + 4 * blocks_sent
    sat = by_groups(saturation[0, 0])
    cell_list = by_groups(cell_send[0, 0])
    halves = cell_list.shape[0] // 4
    groups = sat.shape[0] // 4
    half, single = jnp.bfloat16, jnp.float32

    def like(array):
        return jax.ShapeDtypeStruct(array.shape, array.dtype)

    widened = (extended_blocks, columns, size)
    *packed, guess, sends = call(
        functools.partial(pack_kernel, mesh_dims),
        [jax.ShapeDtypeStruct((halo_rows + tail_rows, size), half)] * 4
        + [like(guess), like(sends)],
        [far] * 4,
        [
            pltpu.VMEM(cell_list.shape, jnp.int32),
            pltpu.VMEM(sat.shape, single),
            pltpu.VMEM((4 * halves, lane_width), single),
            pltpu.SemaphoreType.DMA((3 + blocks,)),
        ],
    )(*map(keep_far, (sends, guess, cell_list, sat)))
    arrived = trade(packed, plans)

    remote = [
        couple,
        inverse,
        by_cells(cell_faces[0, 0]),
        by_cells(face_coeff[0, 0]),
        by_cells(cell_source[0]),
        by_cells(cell_neighbours[0, 0]),
        by_cells(upwind_flags[0, 0]),
        sat,
        by_cells(step_ratio[0]),
        links,
    ]
    (
        couple,
        inverse,
        cell_faces,
        coeff,
        source,
        neighbours,
        flags,
        sat,
        ratio,
        links,
        near0,
        near1,
        own,
        *listed,
    ) = call(
        functools.partial(fetch_kernel, mesh_dims, len(remote)),
        [like(array) for array in remote]
        + [like(sends)] * 2
        + [jax.ShapeDtypeStruct(guess.shape, half)]
        + [
            jax.ShapeDtypeStruct((4 * blocks_sent,) + array.shape[1:], array.dtype)
            for array in (couple, inverse, rhs)
        ],
        [whole, whole] + [far] * (1 + len(remote)),
        [pltpu.SemaphoreType.DMA((len(remote) + 4 * blocks_sent,))],
        traffic=4 * guess.size,
    )(guess, sends, *map(keep_far, [rhs] + remote))

    sweep_flops = 6 * blocks * columns * size * size
    extended, *packed = call(
        functools.partial(first_edge_kernel, mesh_dims),
        [jax.ShapeDtypeStruct(widened, half)]
        + [jax.ShapeDtypeStruct((halo_rows, size), half)] * 4,
        [whole] * 10,
        flops=sweep_flops // 2,
    )(near0, near1, own, *(arrived[k] for k in (1, 0, 2, 3)), *listed)
    swept = trade(packed, plans)

    tails = [piece[halo_rows:] for piece in arrived]
    cell_rows = -(-(groups + halves) // 8) * 8
    own, across = call(
        functools.partial(first_sweep_kernel, mesh_dims, halves),
        [like(own), jax.ShapeDtypeStruct(neighbours.shape, single)],
        [whole] * 11,
        [pltpu.VMEM((6 * cell_rows, lane_width), single)],
        sweep_flops,
    )(links, extended, couple, inverse, rhs, sat, neighbours, *tails)

    packed = call(
        functools.partial(second_edge_kernel, mesh_dims),
        [jax.ShapeDtypeStruct((tail_rows, size), half)] * 4,
        [whole] * 10,
        [pltpu.VMEM((extended_blocks, tail_rows, size), half)],
        sweep_flops // 16,
    )(near0, near1, own, *(swept[k] for k in (1, 0, 2, 3)), *listed)
    edges = trade(packed, plans)

    traces, partial = call(
        functools.partial(second_sweep_kernel, mesh_dims, blocks_sent),
        [jax.ShapeDtypeStruct(guess.shape, single), jax.ShapeDtypeStruct(coeff.shape, single)],
        [whole] * 10,
        [
            pltpu.VMEM(widened, half),
            pltpu.VMEM(guess.shape, single),
            pltpu.VMEM((blocks, size), single),
            pltpu.SemaphoreType.DMA((blocks,)),
        ],
        sweep_flops,
        out_specs=[far, whole],
    )(links, own, *(swept[k] for k in (1, 0, 2, 3)), couple, inverse, rhs, cell_faces)

    (following,) = call(
        functools.partial(cells_kernel, mesh_dims, blocks, blocks_sent),
        [like(sat)],
        [whole] * 12,
        [pltpu.VMEM((4 * blocks_sent, lane_width), single)],
    )(partial, *(edges[k] for k in (1, 3, 0, 2)), across, cell_faces, coeff, source, flags, sat, ratio)
    saturation_next = jnp.swapaxes(following.reshape(groups, 4, lane_width), 0, 1).reshape(4, -1)
    return traces[None, None], saturation_next[None, None]


def solution(mesh):
    mesh_dims = (mesh.shape["wide"], mesh.shape["narrow"])

    def spec(rank):
        return P("wide", "narrow", *([None] * (rank - 2)))

    placed = tuple(spec(rank) for rank in (5, 5, 5, 6, 4, 4, 4, 4, 3, 4, 4, 4, 4, 3))
    return jax.shard_map(
        functools.partial(per_device, mesh_dims, pairings(*mesh_dims)),
        mesh=mesh,
        in_specs=placed,
        out_specs=(spec(5), spec(4)),
        check_vma=False,
    )
```

```python
import functools

import jax
import jax.numpy as jnp
from jax import lax
from jax.experimental import pallas as pl
from jax.experimental.pallas import tpu as pltpu
from jax.sharding import PartitionSpec as P

lane_width = 128
tail_rows = 16
vmem_bytes = 24 * 1024 * 1024
axes = ("wide", "narrow")


def pairings(wide, narrow):
    def number(i, j):
        return i * narrow + j

    def close(pairs, partner_of):
        taken = {d for pair in pairs for d in pair}
        for i in range(wide):
            for j in range(narrow):
                partner = partner_of(i, j)
                if number(i, j) in taken:
                    continue
                if 0 <= partner[0] < wide and 0 <= partner[1] < narrow:
                    if number(*partner) not in taken:
                        pairs.append((number(i, j), number(*partner)))
                        taken |= {number(i, j), number(*partner)}
        moves = [(a, b) for a, b in pairs] + [(b, a) for a, b in pairs if a != b]
        sources = {a for a, _ in moves}
        return moves + [(d, d) for d in range(wide * narrow) if d not in sources]

    plans = []
    for first in (0, 1):
        pairs = [
            (number(i, j), number(i + 1, j))
            for i in range(first, wide - 1, 2)
            for j in range(narrow)
        ]
        plans.append(close(pairs, lambda i, j: (i, j ^ 1)))
    for first in (0, 1):
        pairs = [
            (number(i, j), number(i, j + 1))
            for i in range(wide)
            for j in range(first, narrow - 1, 2)
        ]
        plans.append(close(pairs, lambda i, j: (i, narrow - 1 - j)))
    return plans


def trade(pieces, plans):
    return [lax.ppermute(piece, axes, plan) for piece, plan in zip(pieces, plans)]


def sides_of(wide, narrow):
    found = []
    for base, axis, count in ((0, "wide", wide), (2, "narrow", narrow)):
        here = lax.axis_index(axis)
        for first in (0, 1):
            partner = ((here + first) ^ 1) - first
            side = base + jnp.where(partner > here, 1, 0)
            found.append((side, (partner >= 0) & (partner < count)))
    return found


def spread(row):
    return jnp.broadcast_to(row, (8, lane_width))


def take_lanes(row, low):
    return jnp.take_along_axis(row, low, axis=1, mode="promise_in_bounds")


def pack_kernel(
    mesh_dims, sends_far, guess_far, list_far, sat_far,
    out0, out1, out2, out3, guess, sends,
    cell_list, sat, picked, arrivals,
):
    places = sides_of(*mesh_dims)
    blocks, size = guess.shape[0], guess.shape[1]
    copies = [
        pltpu.make_async_copy(far, near, arrivals.at[slot])
        for slot, (far, near) in enumerate(
            ((list_far, cell_list), (sat_far, sat), (sends_far, sends))
        )
    ]
    loads = [
        pltpu.make_async_copy(guess_far.at[block], guess.at[block], arrivals.at[3 + block])
        for block in range(blocks)
    ]
    for copy in copies + loads:
        copy.start()
    for copy in copies:
        copy.wait()
    blocks_sent = sends.shape[0]
    groups = sat.shape[0] // 4
    lists = cell_list.shape[0]
    halves = lists // 4
    index = cell_list[...]
    high = index >> 7
    low = index & (lane_width - 1)
    found = jnp.zeros(index.shape, jnp.float32)
    for group in range(groups):
        modes = sat[pl.ds(group * 4, 4), :]
        mean, along_x, along_y = modes[0:1], modes[1:2], modes[2:3]
        four = jnp.concatenate([mean - along_x, mean + along_x, mean - along_y, mean + along_y], 0)
        rows = jnp.concatenate([four] * halves, 0)
        found = jnp.where(high == group, take_lanes(rows, low), found)
    picked[...] = found
    for (side, _), out in zip(places, (out0, out1, out2, out3)):
        values = [picked[pl.ds(half * 4 + side, 1), :] for half in range(halves)]
        coarse = [value.astype(jnp.bfloat16).astype(jnp.float32) for value in values]
        fine = [value - rounded for value, rounded in zip(values, coarse)]
        blank = jnp.zeros((tail_rows - 2 * halves, lane_width), jnp.float32)
        out[pl.ds(blocks_sent * size, tail_rows), :] = jnp.concatenate(
            coarse + fine + [blank], 0
        ).astype(jnp.bfloat16)
    listed = listed_blocks(sends, places)
    for load in loads:
        load.wait()
    for picks, out in zip(listed, (out0, out1, out2, out3)):
        for slot, block in enumerate(picks):
            out[pl.ds(slot * size, size), :] = guess[block].astype(jnp.bfloat16)


def listed_blocks(sends, places):
    value = sends[...]
    count = value.shape[0]
    sides = [[value[slot, side] for slot in range(count)] for side in range(4)]
    found = []
    for pairing, (side, _) in enumerate(places):
        first = 0 if pairing < 2 else 2
        found.append(
            [jnp.where(side == first, a, b) for a, b in zip(sides[first], sides[first + 1])]
        )
    return found


def listed_links(near0, near1):
    values = near0[...], near1[...]
    slots, pairings = values[0].shape
    return [
        [value[slot, pairing] for value in values]
        for pairing in range(pairings)
        for slot in range(slots)
    ]


def linked_blocks(links):
    value = links[...]
    return [[value[k, block] for k in range(2)] for block in range(value.shape[1])]


def in_parts(links):
    pairs = linked_blocks(links)
    for start in range(0, len(pairs), 8):
        yield range(start, min(start + 8, len(pairs))), pairs[start : start + 8]


def fetch_kernel(mesh_dims, count, guess, sends, rhs_far, *refs):
    fars, nears = refs[:count], refs[count : 2 * count]
    near0, near1, extended, couple_listed, inverse_listed, rhs_listed, arrivals = refs[2 * count :]
    listed = sends[...]
    columns = []
    for pairing, (side, _) in enumerate(sides_of(*mesh_dims)):
        first = 0 if pairing < 2 else 2
        columns.append(
            jnp.where(side == first, listed[:, first : first + 1], listed[:, first + 1 : first + 2])
        )
    listed = jnp.concatenate(columns, 1)
    slots, pairings = listed.shape
    blocks = [listed[slot, pairing] for pairing in range(pairings) for slot in range(slots)]
    copies = [
        pltpu.make_async_copy(far, near, arrivals.at[slot])
        for slot, (far, near) in enumerate(zip(fars, nears))
    ] + [
        pltpu.make_async_copy(rhs_far.at[block], rhs_listed.at[place], arrivals.at[count + place])
        for place, block in enumerate(blocks)
    ]
    for copy in copies:
        copy.start()
    for block in range(guess.shape[0]):
        extended[block] = guess[block].astype(jnp.bfloat16)
    for copy in copies:
        copy.wait()
    couple, inverse, links = nears[0], nears[1], nears[-1][...]
    for place, block in enumerate(blocks):
        couple_listed[place] = couple[block]
        inverse_listed[place] = inverse[block]
    for k, near in enumerate((near0, near1)):
        chosen = jnp.zeros_like(listed)
        for block in range(links.shape[1]):
            chosen = jnp.where(listed == block, links[k, block], chosen)
        near[...] = chosen


def product(left, right):
    return lax.dot_general(
        left, right, (((1,), (1,)), ((), ())), preferred_element_type=jnp.float32
    )


def relax(extended, couple, inverse, rhs, blocks, links, rows):
    resid = []
    for block, pair in zip(blocks, links):
        near = jnp.concatenate([extended[link, 0:rows, :] for link in pair], 1)
        matrix = jnp.concatenate([couple[block, k] for k in range(len(pair))], 1)
        resid.append((rhs[block, 0:rows, :] - product(near, matrix)).astype(jnp.bfloat16))
    return [product(part, inverse[block]) for part, block in zip(resid, blocks)]


def land(extended, places, arrived, blocks_sent, rows):
    own_count = extended.shape[0] - 4 * blocks_sent
    size = extended.shape[1]
    for (side, exists), came in zip(places, arrived):
        for block in range(blocks_sent):
            value = came[pl.ds(block * size, rows), :]
            value = jnp.where(exists, value, jnp.zeros_like(value))
            extended[own_count + side * blocks_sent + block, 0:rows, :] = value


def first_edge_kernel(
    mesh_dims, near0, near1, _, in1, in0, in2, in3, couple, inverse, rhs,
    extended, out0, out1, out2, out3,
):
    size = extended.shape[1]
    slots = near0.shape[0]
    links = listed_links(near0, near1)
    land(extended, sides_of(*mesh_dims), (in0, in1, in2, in3), slots, size)
    fresh = relax(extended, couple, inverse, rhs, range(len(links)), links, size)
    for pairing, out in enumerate((out0, out1, out2, out3)):
        for slot in range(slots):
            value = fresh[pairing * slots + slot]
            out[pl.ds(slot * size, size), :] = value.astype(jnp.bfloat16)


def spread_rows(table, first_row, count):
    return [spread(table[pl.ds(first_row + row, 1), :]) for row in range(count)]


def look_up(rows, high, low, value, numbers=None):
    for number, row in zip(numbers or range(len(rows)), rows):
        value = jnp.where(high == number, take_lanes(row, low), value)
    return value


def nothing():
    return jnp.zeros((8, lane_width), jnp.float32)


def first_sweep_kernel(
    mesh_dims, halves, links, extended, couple, inverse, rhs,
    sat, neighbours, tail0, tail1, tail2, tail3,
    smoothed, across, across_rows,
):
    places = sides_of(*mesh_dims)
    groups = sat.shape[0] // 4
    stride = across_rows.shape[0] // 6
    modes = [sat[pl.ds(mode, groups, stride=4), :] for mode in range(4)]
    for (side, exists), came in zip(places, (tail0, tail1, tail2, tail3)):
        value = came[...].astype(jnp.float32)
        value = value[0:halves] + value[halves : 2 * halves]
        value = jnp.where(exists, value, jnp.zeros_like(value))
        for half in range(halves):
            across_rows[pl.ds(side * stride + groups + half, 1), :] = value[half : half + 1]
    for face in range(6):
        mode = modes[face // 2 + 1]
        across_rows[pl.ds(face * stride, groups), :] = (
            modes[0] + mode if face % 2 == 0 else modes[0] - mode
        )
    for face in range(6):
        rows = spread_rows(across_rows, face * stride, groups + halves if face < 4 else groups)
        for start in range(0, groups, 8):
            index = neighbours[pl.ds(face * groups + start, 8), :]
            high, low = index >> 7, index & (lane_width - 1)
            if 0 < face < 4:
                high = jnp.where(high >= groups, high - face * halves, high)
            across[pl.ds(face * groups + start, 8), :] = look_up(rows, high, low, nothing())
    for blocks, pairs in in_parts(links):
        fresh = relax(extended, couple, inverse, rhs, blocks, pairs, extended.shape[1])
        for block, value in zip(blocks, fresh):
            smoothed[block] = value.astype(jnp.bfloat16)


def second_edge_kernel(
    mesh_dims, near0, near1, _, in1, in0, in2, in3, couple, inverse, rhs,
    extended, out0, out1, out2, out3,
):
    slots = near0.shape[0]
    links = listed_links(near0, near1)
    land(extended, sides_of(*mesh_dims), (in0, in1, in2, in3), slots, tail_rows)
    fresh = relax(extended, couple, inverse, rhs, range(len(links)), links, tail_rows)
    for pairing, out in enumerate((out0, out1, out2, out3)):
        rows = [fresh[pairing * slots + slot][0:1, :] for slot in range(slots)]
        blank = jnp.zeros((tail_rows - len(rows), lane_width), jnp.float32)
        out[...] = jnp.concatenate(rows + [blank], 0).astype(jnp.bfloat16)


def second_sweep_kernel(
    mesh_dims, blocks_sent, links, _, in0, in1, in2, in3, couple, inverse, rhs, cell_faces,
    traces, partial, extended, fresh, column, departures,
):
    land(extended, sides_of(*mesh_dims), (in0, in1, in2, in3), blocks_sent, extended.shape[1])
    stores = []
    for blocks, pairs in in_parts(links):
        values = relax(extended, couple, inverse, rhs, blocks, pairs, extended.shape[1])
        for block, value in zip(blocks, values):
            fresh[block] = value
            stores.append(
                pltpu.make_async_copy(fresh.at[block], traces.at[block], departures.at[block])
            )
            stores[block].start()
            column[pl.ds(block, 1), :] = value[0:1].astype(jnp.bfloat16).astype(jnp.float32)
    rows = spread_rows(column, 0, column.shape[0])
    for start in range(0, cell_faces.shape[0], 8):
        index = cell_faces[pl.ds(start, 8), :]
        partial[pl.ds(start, 8), :] = look_up(
            rows, index >> 7, index & (lane_width - 1), nothing()
        )
    for store in stores:
        store.wait()


def cells_kernel(
    mesh_dims, blocks, blocks_sent, partial, in1, in3, in0, in2, across,
    cell_faces, coeff, source, flags, sat, ratio, out,
):
    places = sides_of(*mesh_dims)
    groups = sat.shape[0] // 4
    edge_rows, numbers = [], []
    for (side, exists), came in zip(places, (in0, in1, in2, in3)):
        value = came[...].astype(jnp.float32)[0:blocks_sent]
        value = jnp.where(exists, value, jnp.zeros_like(value))
        for block in range(blocks_sent):
            edge_rows.append(spread(value[block : block + 1]))
            numbers.append(side * blocks_sent + block)
    modes = [sat[pl.ds(mode, groups, stride=4), :] for mode in range(4)]
    weights = [coeff[pl.ds(face * groups, groups), :] for face in range(6)]
    traces = []
    for face in range(6):
        parts = []
        for start in range(0, groups, 8):
            rows = pl.ds(face * groups + start, 8)
            index = cell_faces[rows, :]
            high, low = (index >> 7) - blocks, index & (lane_width - 1)
            parts.append(look_up(edge_rows, high, low, partial[rows, :], numbers))
        traces.append(jnp.concatenate(parts, 0))
    total = weights[0]
    gained = source[...] + weights[0] * traces[0]
    for face in range(1, 6):
        total = total + weights[face]
        gained = gained + weights[face] * traces[face]
    pressure = gained / total
    flux = [weights[face] * (pressure - traces[face]) for face in range(6)]
    flow = []
    for face in range(6):
        mode = modes[face // 2 + 1]
        own = modes[0] - mode if face % 2 == 0 else modes[0] + mode
        rows = pl.ds(face * groups, groups)
        flow.append(flux[face] * jnp.where(flags[rows, :] == 1, own, across[rows, :]))
    step = ratio[...]
    out[pl.ds(0, groups, stride=4), :] = modes[0] - step * (
        flow[0] + flow[1] + flow[2] + flow[3] + flow[4] + flow[5]
    )
    for mode in range(1, 4):
        lo, hi = 2 * mode - 2, 2 * mode - 1
        volume = 0.5 * (flux[hi] - flux[lo]) * modes[0]
        out[pl.ds(mode, groups, stride=4), :] = modes[mode] + 3.0 * step * (
            volume - (flow[hi] - flow[lo])
        )


whole = pl.BlockSpec(memory_space=pltpu.VMEM)
far = pl.BlockSpec(memory_space=pl.ANY)


def call(kernel, outs, specs, scratch=(), flops=0, traffic=0, out_specs=None, aliases=None):
    return pl.pallas_call(
        kernel,
        out_shape=outs,
        in_specs=specs,
        out_specs=[whole] * len(outs) if out_specs is None else out_specs,
        scratch_shapes=list(scratch),
        input_output_aliases=aliases or {},
        compiler_params=pltpu.CompilerParams(vmem_limit_bytes=vmem_bytes),
        cost_estimate=pl.CostEstimate(flops=flops, bytes_accessed=traffic, transcendentals=0),
    )


def keep_near(array):
    return pltpu.with_memory_space_constraint(array, pltpu.VMEM)


def keep_far(array):
    return pltpu.with_memory_space_constraint(array, pltpu.HBM)


def by_cells(array):
    return array.reshape(-1, lane_width)


def by_groups(array):
    rows = array.shape[0]
    return jnp.swapaxes(array.reshape(rows, -1, lane_width), 0, 1).reshape(-1, lane_width)


def per_device(
    mesh_dims,
    plans,
    trace_guess,
    trace_rhs,
    block_inverse,
    coupling,
    block_neighbours,
    block_send,
    cell_faces,
    face_coeff,
    cell_source,
    cell_neighbours,
    upwind_flags,
    cell_send,
    saturation,
    step_ratio,
):
    guess = trace_guess[0, 0]
    rhs = trace_rhs[0, 0]
    inverse = block_inverse[0, 0]
    couple = coupling[0, 0]
    links = block_neighbours[0, 0].T
    sends = block_send[0, 0].T
    blocks, columns, size = guess.shape
    blocks_sent = sends.shape[0]
    halo_rows = blocks_sent * columns
    extended_blocks = blocks + 4 * blocks_sent
    sat = by_groups(saturation[0, 0])
    cell_list = by_groups(cell_send[0, 0])
    halves = cell_list.shape[0] // 4
    groups = sat.shape[0] // 4
    half, single = jnp.bfloat16, jnp.float32

    def like(array):
        return jax.ShapeDtypeStruct(array.shape, array.dtype)

    widened = (extended_blocks, columns, size)
    *packed, guess, sends = call(
        functools.partial(pack_kernel, mesh_dims),
        [jax.ShapeDtypeStruct((halo_rows + tail_rows, size), half)] * 4
        + [like(guess), like(sends)],
        [far] * 4,
        [
            pltpu.VMEM(cell_list.shape, jnp.int32),
            pltpu.VMEM(sat.shape, single),
            pltpu.VMEM((4 * halves, lane_width), single),
            pltpu.SemaphoreType.DMA((3 + blocks,)),
        ],
    )(*map(keep_far, (sends, guess, cell_list, sat)))
    arrived = trade(packed, plans)

    remote = [
        couple,
        inverse,
        by_cells(cell_faces[0, 0]),
        by_cells(face_coeff[0, 0]),
        by_cells(cell_source[0]),
        by_cells(cell_neighbours[0, 0]),
        by_cells(upwind_flags[0, 0]),
        sat,
        by_cells(step_ratio[0]),
        links,
    ]
    (
        couple,
        inverse,
        cell_faces,
        coeff,
        source,
        neighbours,
        flags,
        sat,
        ratio,
        links,
        near0,
        near1,
        extended,
        *listed,
    ) = call(
        functools.partial(fetch_kernel, mesh_dims, len(remote)),
        [like(array) for array in remote]
        + [like(sends)] * 2
        + [jax.ShapeDtypeStruct(widened, half)]
        + [
            jax.ShapeDtypeStruct((4 * blocks_sent,) + array.shape[1:], array.dtype)
            for array in (couple, inverse, rhs)
        ],
        [whole, whole] + [far] * (1 + len(remote)),
        [pltpu.SemaphoreType.DMA((len(remote) + 4 * blocks_sent,))],
        traffic=4 * guess.size,
    )(guess, sends, *map(keep_far, [rhs] + remote))

    sweep_flops = 6 * blocks * columns * size * size
    extended, *packed = call(
        functools.partial(first_edge_kernel, mesh_dims),
        [like(extended)] + [jax.ShapeDtypeStruct((halo_rows, size), half)] * 4,
        [whole] * 10,
        flops=sweep_flops // 2,
        aliases={2: 0},
    )(near0, near1, keep_near(extended), *(arrived[k] for k in (1, 0, 2, 3)), *listed)
    swept = trade(packed, plans)

    tails = [piece[halo_rows:] for piece in arrived]
    cell_rows = -(-(groups + halves) // 8) * 8
    extended, across = call(
        functools.partial(first_sweep_kernel, mesh_dims, halves),
        [like(extended), jax.ShapeDtypeStruct(neighbours.shape, single)],
        [whole] * 11,
        [pltpu.VMEM((6 * cell_rows, lane_width), single)],
        sweep_flops,
    )(links, extended, couple, inverse, rhs, sat, neighbours, *tails)

    extended, *packed = call(
        functools.partial(second_edge_kernel, mesh_dims),
        [like(extended)] + [jax.ShapeDtypeStruct((tail_rows, size), half)] * 4,
        [whole] * 10,
        flops=sweep_flops // 16,
        aliases={2: 0},
    )(near0, near1, keep_near(extended), *(swept[k] for k in (1, 0, 2, 3)), *listed)
    edges = trade(packed, plans)

    traces, partial, _ = call(
        functools.partial(second_sweep_kernel, mesh_dims, blocks_sent),
        [
            jax.ShapeDtypeStruct(guess.shape, single),
            jax.ShapeDtypeStruct(coeff.shape, single),
            like(extended),
        ],
        [whole] * 10,
        [
            pltpu.VMEM(guess.shape, single),
            pltpu.VMEM((blocks, size), single),
            pltpu.SemaphoreType.DMA((blocks,)),
        ],
        sweep_flops,
        out_specs=[far, whole, whole],
        aliases={1: 2},
    )(links, keep_near(extended), *swept, couple, inverse, rhs, cell_faces)

    (following,) = call(
        functools.partial(cells_kernel, mesh_dims, blocks, blocks_sent),
        [like(sat)],
        [whole] * 12,
    )(partial, *(edges[k] for k in (1, 3, 0, 2)), across, cell_faces, coeff, source, flags, sat, ratio)
    saturation_next = jnp.swapaxes(following.reshape(groups, 4, lane_width), 0, 1).reshape(4, -1)
    return traces[None, None], saturation_next[None, None]


def solution(mesh):
    mesh_dims = (mesh.shape["wide"], mesh.shape["narrow"])

    def spec(rank):
        return P("wide", "narrow", *([None] * (rank - 2)))

    placed = tuple(spec(rank) for rank in (5, 5, 5, 6, 4, 4, 4, 4, 3, 4, 4, 4, 4, 3))
    return jax.shard_map(
        functools.partial(per_device, mesh_dims, pairings(*mesh_dims)),
        mesh=mesh,
        in_specs=placed,
        out_specs=(spec(5), spec(4)),
        check_vma=False,
    )
```
